256 devices in a mesh: lat: 8 (over x, y_hi), lon: 32 (over y_lo, z, core).
Axes of the slice: x: 4, y: 4 (y_hi: 2, y_lo: 2; y = y_hi * 2 + y_lo), z: 8, core: 2. Of those that a mesh axis runs over, the one named last changes fastest.
Arguments:
- tokens: bfloat16 [96, 384, 4, 512], P('lat', 'lon'), may hold values from -6 to 6
- norm_attn: float32 [512], replicated, may hold values from 0.1 to 1.9
- w_qkv: bfloat16 [512, 1536], replicated, may hold values from -0.25 to 0.25
- pos_bias: float32 [16, 144, 144], replicated, may hold values from -4 to 400
- w_out: bfloat16 [512, 512], replicated, may hold values from -0.25 to 0.25
- norm_mlp: float32 [512], replicated, may hold values from 0.1 to 1.9
- w_up: bfloat16 [512, 2048], replicated, may hold values from -0.25 to 0.25
- w_down: bfloat16 [2048, 512], replicated, may hold values from -0.125 to 0.125
- norm_merge: float32 [2048], replicated, may hold values from 0.1 to 1.9
- w_merge: bfloat16 [2048, 1024], P(None, 'lon'), may hold values from -0.125 to 0.125
Outputs:
- merged: bfloat16 [48, 192, 4, 1024], P('lat', None, None, 'lon')
The draws below stay inside these ranges and needn't reach their ends.
All inputs are finite; a program needn't handle non-finite values.
Results may differ from the reference program's by a relative error of at most 0.015.
Values may be sent and summed in bfloat16 or wider, within the bound.
No kernel may reach another device: no remote copies, remote signals or barrier semaphores. Data moves between devices by JAX's collectives and lax.ppermute only.
A program may use at most 128 MiB of HBM per device.

```python
import jax
import jax.numpy as jnp
from jax import lax

D = 512
HEADS = 16
FFN = 2048
MERGED = 1024
LEV = 4
WIN_LAT = 6
WIN_LON = 12
WIN_LEV = 2
HEAD_DIM = 32
WIN_TOK = 144
LAT_ALL = 96
LON_ALL = 384


def draw_pos_bias(key, part):
    key = jax.random.fold_in(key, 11)
    key_base = jax.random.fold_in(key, 0)
    shape = (HEADS, WIN_TOK, WIN_TOK)
    return jnp.clip(jax.random.normal(key_base, shape, jnp.float32), -4.0, 4.0)


def block_levels(rng, extent, cuts, low, largest):
    loudness = 1.0
    for dim, blocks in cuts:
        steps = jax.random.uniform(jax.random.fold_in(jax.random.fold_in(rng, 6), dim), (blocks,), jnp.float32, low / len(cuts), largest / len(cuts))
        loudness = loudness * jnp.repeat(jnp.exp(steps), extent[dim] // blocks).reshape((-1,) + (1,) * (len(extent) - 1 - dim))
    return loudness


def scatter_about(key, dims, deviation, most, cuts=(), kind=jnp.bfloat16):
    level = block_levels(key, dims, cuts, -0.22, 0.18) if cuts else 1.0
    values = jax.random.normal(key, dims, jnp.float32) * deviation * level
    return jnp.minimum(jnp.maximum(values, -most), most).astype(kind)


def setup_inputs(seed: int = 0) -> dict:
    arg_keys = jax.random.split(jax.random.key(seed), 11)
    return {
        "tokens": scatter_about(arg_keys[0], (LAT_ALL, LON_ALL, LEV, D), 1.0, 6.0, ((0, 8), (1, 32))),
        "norm_attn": jnp.clip(1.0 + 0.18 * jax.random.normal(arg_keys[1], (D,), jnp.float32), 0.1, 1.9),
        "w_qkv": scatter_about(arg_keys[2], (D, 3 * D), D ** -0.5, 0.25),
        "pos_bias": draw_pos_bias(jax.random.fold_in(arg_keys[10], 71), 0),
        "w_out": scatter_about(arg_keys[4], (D, D), D ** -0.5, 0.25),
        "norm_mlp": jnp.clip(1.0 + 0.18 * jax.random.normal(arg_keys[5], (D,), jnp.float32), 0.1, 1.9),
        "w_up": scatter_about(arg_keys[6], (D, FFN), D ** -0.5, 0.25),
        "w_down": scatter_about(arg_keys[7], (FFN, D), FFN ** -0.5, 0.125),
        "norm_merge": jnp.clip(1.0 + 0.18 * jax.random.normal(arg_keys[8], (4 * D,), jnp.float32), 0.1, 1.9),
        "w_merge": scatter_about(arg_keys[9], (4 * D, MERGED), (4 * D) ** -0.5, 0.125, ((1, 32),)),
    }


EPS = 1e-05

def layer_norm(values, gain):
    mean = lax.optimization_barrier(jnp.mean(values, axis=-1, keepdims=True))
    centred = values - mean
    spread = lax.optimization_barrier(jnp.mean(centred * centred, axis=-1, keepdims=True))
    return centred * lax.rsqrt(spread + EPS) * gain

def to_windows(grid):
    rows, cols, levels, width = grid.shape
    shaped = grid.reshape(rows // WIN_LAT, WIN_LAT, cols // WIN_LON, WIN_LON, levels // WIN_LEV, WIN_LEV, width)
    return shaped.transpose(0, 2, 4, 1, 3, 5, 6).reshape(-1, WIN_TOK, width)

def from_windows(windows, rows, cols, levels):
    width = windows.shape[-1]
    shaped = windows.reshape(rows // WIN_LAT, cols // WIN_LON, levels // WIN_LEV, WIN_LAT, WIN_LON, WIN_LEV, width)
    return shaped.transpose(0, 3, 1, 4, 2, 5, 6).reshape(rows, cols, levels, width)

def attend(windows, allowed, norm_attn, w_qkv, pos_bias, w_out):
    count = windows.shape[0]
    flat = windows.reshape(count * WIN_TOK, D)
    normed = layer_norm(flat.astype(jnp.float32), norm_attn).astype(jnp.bfloat16)
    qkv = jnp.dot(normed, w_qkv, preferred_element_type=jnp.float32).astype(jnp.bfloat16)
    qkv = qkv.reshape(count, WIN_TOK, 3, HEADS, HEAD_DIM)
    query = qkv[:, :, 0].astype(jnp.float32)
    keys = qkv[:, :, 1].astype(jnp.float32)
    values = qkv[:, :, 2].astype(jnp.float32)
    scores = jnp.einsum('nqhd,nkhd->nhqk', query, keys) * HEAD_DIM ** (-0.5) + pos_bias[None]
    scores = jnp.where(allowed[:, None], scores, -1e+30)
    highest = lax.optimization_barrier(jnp.max(scores, axis=-1, keepdims=True))
    expd = jnp.exp(scores - highest)
    weights = (expd / lax.optimization_barrier(jnp.sum(expd, axis=-1, keepdims=True))).astype(jnp.bfloat16)
    mixed = jnp.einsum('nhqk,nkhd->nqhd', weights.astype(jnp.float32), values).astype(jnp.bfloat16)
    update = jnp.dot(mixed.reshape(count * WIN_TOK, D), w_out, preferred_element_type=jnp.float32)
    return (flat.astype(jnp.float32) + update).astype(jnp.bfloat16).reshape(count, WIN_TOK, D)

def feed_forward(block, norm_mlp, w_up, w_down):
    normed = layer_norm(block.astype(jnp.float32), norm_mlp).astype(jnp.bfloat16)
    hidden = jax.nn.gelu(jnp.dot(normed, w_up, preferred_element_type=jnp.float32), approximate=False).astype(jnp.bfloat16)
    return (block.astype(jnp.float32) + jnp.dot(hidden, w_down, preferred_element_type=jnp.float32)).astype(jnp.bfloat16)

def merge_patches(grid, norm_merge):
    rows, cols, levels, width = grid.shape
    shaped = grid.reshape(rows // 2, 2, cols // 2, 2, levels, width).transpose(0, 2, 4, 3, 1, 5)
    joined = shaped.reshape(rows // 2, cols // 2, levels, 4 * width)
    return layer_norm(joined.astype(jnp.float32), norm_merge).astype(jnp.bfloat16)

def reference(tokens, norm_attn, w_qkv, pos_bias, w_out, norm_mlp, w_up, w_down, norm_merge, w_merge):
    half_lat = WIN_LAT // 2
    half_lon = WIN_LON // 2
    half_lev = WIN_LEV // 2
    padded = jnp.pad(tokens, ((half_lat, half_lat), (0, 0), (0, 0), (0, 0)))
    rolled = jnp.roll(padded, (-half_lon, -half_lev), axis=(1, 2))
    row_total = LAT_ALL + 2 * half_lat
    rows = jnp.arange(row_total, dtype=jnp.int32) - half_lat
    row_ok = (rows >= 0) & (rows < LAT_ALL)
    lev_group = ((jnp.arange(LEV, dtype=jnp.int32) + half_lev) % LEV + half_lev) // WIN_LEV
    tags = jnp.where(row_ok[:, None, None], lev_group[None, None, :], -1).astype(jnp.int32)
    tags = jnp.broadcast_to(tags, (row_total, LON_ALL, LEV))
    band_count = row_total // WIN_LAT
    bands = rolled.reshape(band_count, WIN_LAT, LON_ALL, LEV, D)
    tag_bands = tags.reshape(band_count, WIN_LAT, LON_ALL, LEV)

    def one_band(pair):
        band, tag = pair
        windows = to_windows(band)
        tag_win = to_windows(tag[..., None])[..., 0]
        allowed = tag_win[:, :, None] == tag_win[:, None, :]
        result = attend(windows, allowed, norm_attn, w_qkv, pos_bias, w_out)
        return from_windows(result, WIN_LAT, LON_ALL, LEV)
    attended = lax.map(one_band, (bands, tag_bands)).reshape(row_total, LON_ALL, LEV, D)
    attended = jnp.roll(attended, (half_lon, half_lev), axis=(1, 2))[half_lat:half_lat + LAT_ALL]
    block = lax.map(lambda row: feed_forward(row, norm_mlp, w_up, w_down), attended.reshape(LAT_ALL, LON_ALL * LEV, D))
    block = block.reshape(LAT_ALL, LON_ALL, LEV, D)
    joined = merge_patches(block, norm_merge)
    merged = jnp.dot(joined.reshape(-1, 4 * D), w_merge, preferred_element_type=jnp.float32).astype(jnp.bfloat16)
    return merged.reshape(LAT_ALL // 2, LON_ALL // 2, LEV, MERGED)
```

```python
import functools

import jax
import jax.numpy as jnp
import numpy as np
from jax import lax
from jax.experimental import pallas as pl
from jax.experimental.pallas import tpu as pltpu
from jax.sharding import PartitionSpec as P

HEADS = 16
HEAD_DIM = 32
WIDTH = 512
FFN = 2048
ROWS = 12
HALF = 6
WIN = 144
HALF_WIN = 72
BAND = 288
LOG2E = 1.4426950408889634
EPS = 1e-05
BIG = -1e30
BF = jnp.bfloat16
F32 = jnp.float32
LEVELS = ((1, 2), (3, 0))
MERGE_PAD = 40


def dot(a, b, dims=((1,), (0,))):
    return lax.dot_general(a, b, (dims, ((), ())), preferred_element_type=F32)


NT = ((1,), (1,))


def window_order():
    order = []
    for ihalf in range(2):
        for k in range(2):
            for i3 in range(3):
                for j in range(12):
                    order.append(((ihalf * 3 + i3) * 12 + j) * 2 + k)
    return order


def bias_permutation():
    out = np.zeros((WIN, WIN), np.float32)
    out[np.arange(WIN), window_order()] = 1
    return out


def band_permutation():
    out = np.zeros((BAND, BAND), np.float32)
    n = 0
    for t in range(2):
        for ihalf in range(2):
            for k in range(2):
                for i3 in range(3):
                    for j in range(12):
                        i, half, c = ihalf * 3 + i3, j // 6, j % 6
                        out[n, half * 144 + i * 24 + c * 4 + LEVELS[t][k]] = 1
                        n += 1
    return out


def merge_permutation():
    first = np.zeros((4, 4, MERGE_PAD, BAND), np.float32)
    second = np.zeros((4, 4, MERGE_PAD, BAND), np.float32)
    place = {LEVELS[t][k]: (t, k) for t in range(2) for k in range(2)}
    for dj in range(2):
        for di in range(2):
            for lev in range(4):
                t, k = place[lev]
                for b in range(6):
                    for a in range(6):
                        r, j = 2 * a + di, 2 * b + dj
                        row = (dj * 2 + di, lev, b * 6 + a)
                        if 3 <= r < 9:
                            i = r - 3
                            first[row + (t * 144 + (i // 3) * 72 + k * 36 + (i % 3) * 12 + j,)] = 1
                        else:
                            band = int(r >= 9)
                            i3 = r - 9 if band else r
                            second[row + ((band * 2 + t) * 72 + k * 36 + i3 * 12 + j,)] = 1
    shape = (4, 4 * MERGE_PAD, BAND)
    return first.reshape(shape), second.reshape(shape)


def normalise(x, gain):
    mean = jnp.sum(x, axis=-1, keepdims=True) * (1.0 / WIDTH)
    centred = x - mean
    spread = jnp.sum(centred * centred, axis=-1, keepdims=True) * (1.0 / WIDTH)
    return centred * lax.rsqrt(spread + EPS) * gain


def split3(x):
    hi = x.astype(BF)
    rest = x - hi.astype(F32)
    mid = rest.astype(BF)
    return hi, mid, (rest - mid.astype(F32)).astype(BF)


def prepare_kernel(bias_ref, wqkv_ref, perm_ref, eye_ref, bias_out, wvt_out):
    perm = perm_ref[...]

    def head(h, carry):
        b = bias_ref[h] * LOG2E
        y = sum(dot(perm, part, NT) for part in split3(b))
        bias_out[h] = sum(dot(part, perm, NT) for part in split3(y))
        return carry

    lax.fori_loop(0, HEADS, head, 0, unroll=4)
    wvt_out[...] = dot(eye_ref[...], wqkv_ref[:, 2 * WIDTH :], NT).astype(BF)


def attend_window(x, normed, q, k, vt_ref, mixt_ref, bias_ref, kaug, qaug, wvt, q_from, q_count):
    q = q[q_from : q_from + q_count].astype(BF)
    k = k.astype(BF)
    vt_ref[...] = dot(wvt, normed, NT).astype(BF)
    lane = lax.broadcasted_iota(jnp.int32, (q_count, 128), 1) // HEAD_DIM
    for h in range(HEADS):
        tile = slice(h // 4 * 128, h // 4 * 128 + 128)
        kx = jnp.concatenate([k[:, tile], kaug], axis=1)
        qm = jnp.where(lane == h % 4, q[:, tile], jnp.zeros((), BF))
        qx = jnp.concatenate([qm, qaug], axis=1)
        s = dot(kx, qx, NT) + bias_ref[h, :, q_from : q_from + q_count]
        p = jnp.exp2(s - jnp.max(s, axis=0, keepdims=True))
        total = jnp.sum(p, axis=0, keepdims=True)
        rows = slice(h * HEAD_DIM, (h + 1) * HEAD_DIM)
        o = dot(vt_ref[rows, :], p.astype(BF))
        mixt_ref[rows, :] = (o * (1.0 / total)).astype(BF)


def feed_forward(attended, norm_mlp, up_ref, down_ref):
    normed = normalise(attended, norm_mlp).astype(BF)
    acc = attended
    step = 512
    for c in range(0, FFN, step):
        h = dot(normed, up_ref[:, c : c + step])
        h = 0.5 * h * (1.0 + lax.erf(h * 0.7071067811865476))
        acc = acc + dot(h.astype(BF), down_ref[c : c + step, :])
    return acc


def group_lanes(count):
    row = lax.broadcasted_iota(jnp.int32, (count, 128), 0)
    lane = lax.broadcasted_iota(jnp.int32, (count, 128), 1)
    return (row % HALF_WIN) // 36, row // HALF_WIN, lane


class Copies:
    def __init__(self, sems):
        self.sems = sems
        self.made = {}

    def start(self, name, src, dst):
        copy = pltpu.make_async_copy(src, dst, self.sems.at[len(self.made)])
        copy.start()
        self.made[name] = copy

    def wait(self, name):
        self.made[name].wait()


def middle_kernel(
    left_ref, right_ref, perm_ref, eye_ref, ga_ref, gm_ref, wqkv_hbm, wvt_hbm, bias_hbm, wout_hbm, up_hbm, down_hbm,
    out_ref, wqk_ref, wvt_ref, bias_ref, wout_ref, up_ref, down_ref, vt_ref, mixt_ref, sems,
):
    copies = Copies(sems)
    copies.start("qk", wqkv_hbm.at[:, : 2 * WIDTH], wqk_ref)
    copies.start("v", wvt_hbm, wvt_ref)
    copies.start("bias", bias_hbm, bias_ref)
    copies.start("out", wout_hbm, wout_ref)
    copies.start("up", up_hbm, up_ref)
    copies.start("down", down_hbm, down_ref)
    x = dot(perm_ref[0], left_ref[...]) + dot(perm_ref[1], right_ref[...])
    normed = normalise(x, ga_ref[...]).astype(BF)
    copies.wait("qk")
    qk = dot(normed, wqk_ref[...])
    q = qk[:, :WIDTH] * (LOG2E * HEAD_DIM**-0.5)
    k = qk[:, WIDTH:]
    group, _, lane = group_lanes(WIN)
    qaug = jnp.where(lane == group, 1.0, 0.0).astype(BF)
    copies.wait("v")
    copies.wait("bias")
    pieces = []
    for t in range(2):
        rows = slice(t * WIN, (t + 1) * WIN)
        kaug = jnp.where((lane < 2) & (lane != group), BIG if t else 0.0, 0.0).astype(BF)
        attend_window(
            x, normed[rows], q[rows], k[rows], vt_ref.at[t], mixt_ref.at[t], bias_ref, kaug, qaug, wvt_ref[...], 0, WIN
        )
        pieces.append(dot(eye_ref[...], mixt_ref[t], NT).astype(BF))
    copies.wait("out")
    update = dot(jnp.concatenate(pieces, axis=0), wout_ref[...])
    attended = (x + update).astype(BF).astype(F32)
    copies.wait("up")
    copies.wait("down")
    out_ref[...] = feed_forward(attended, gm_ref[...], up_ref, down_ref).astype(BF)


def edge_kernel(
    lt_ref, rt_ref, lb_ref, rb_ref, top_ref, bottom_ref, blk1_ref, perm_ref, eye_ref, ga_ref, gm_ref, gg_ref, s1_ref, s2_ref,
    wqkv_hbm, wvt_hbm, bias_hbm, wout_hbm, up_hbm, down_hbm,
    out_ref, wqk_ref, wvt_ref, bias_ref, wout_ref, up_ref, down_ref, vt_ref, mixt_ref, sems,
):
    copies = Copies(sems)
    copies.start("qk", wqkv_hbm.at[:, : 2 * WIDTH], wqk_ref)
    copies.start("v", wvt_hbm, wvt_ref)
    copies.start("bias", bias_hbm, bias_ref)
    copies.start("out", wout_hbm, wout_ref)
    copies.start("up", up_hbm, up_ref)
    copies.start("down", down_hbm, down_ref)
    bands = (
        (top_ref[0], lt_ref[...], top_ref[1], rt_ref[...]),
        (lb_ref[...], bottom_ref[0], rb_ref[...], bottom_ref[1]),
    )
    x = jnp.concatenate([sum(dot(perm_ref[n], piece) for n, piece in enumerate(band)) for band in bands], axis=0)
    normed = normalise(x, ga_ref[...]).astype(BF)
    copies.wait("qk")
    qk = dot(normed, wqk_ref[...])
    q = qk[:, :WIDTH] * (LOG2E * HEAD_DIM**-0.5)
    k = qk[:, WIDTH:]
    group, half, lane = group_lanes(WIN)
    lat = lax.axis_index("lat")
    qgroup, _, qlane = group_lanes(HALF_WIN)
    qaug = jnp.where(qlane == qgroup, 1.0, 0.0).astype(BF)
    copies.wait("v")
    copies.wait("bias")
    pieces = []
    kept = []
    for n in range(2):
        outside = half == n
        off = jnp.where(lat == (lax.axis_size("lat") - 1 if n else 0), BIG, 0.0)
        q_from = 0 if n else HALF_WIN
        for t in range(2):
            w = n * 2 + t
            rows = slice(w * WIN, (w + 1) * WIN)
            other = jnp.where(lane != group, BIG if t else 0.0, 0.0)
            kaug = jnp.where(lane < 2, jnp.where(outside, jnp.minimum(off, other), other), 0.0).astype(BF)
            attend_window(
                x, normed[rows], q[rows], k[rows], vt_ref.at[w], mixt_ref.at[w], bias_ref, kaug, qaug, wvt_ref[...],
                q_from, HALF_WIN,
            )
            pieces.append(dot(eye_ref[...], mixt_ref[w], NT))
            kept.append(x[w * WIN + q_from : w * WIN + q_from + HALF_WIN])
    copies.wait("out")
    update = dot(jnp.concatenate(pieces, axis=0).astype(BF), wout_ref[...])
    attended = (jnp.concatenate(kept, axis=0) + update).astype(BF).astype(F32)
    copies.wait("up")
    copies.wait("down")
    block = feed_forward(attended, gm_ref[...], up_ref, down_ref).astype(BF)
    first = blk1_ref[...]
    patches = [dot(s1_ref[p], first) + dot(s2_ref[p], block) for p in range(4)]
    mean = sum(jnp.sum(v, axis=-1, keepdims=True) for v in patches) * (1.0 / (4 * WIDTH))
    centred = [v - mean for v in patches]
    spread = sum(jnp.sum(v * v, axis=-1, keepdims=True) for v in centred) * (1.0 / (4 * WIDTH))
    scale = lax.rsqrt(spread + EPS)
    for p in range(4):
        out_ref[p] = (centred[p] * scale * gg_ref[p]).astype(BF)


def merge_kernel(own_ref, other_ref, w_ref, out_ref, merged_ref, message_ref):
    core = lax.rem(lax.axis_index("lon"), 2)
    for n, ref in enumerate((own_ref, other_ref)):
        total = sum(dot(ref[p], w_ref[:, p * WIDTH : (p + 1) * WIDTH], NT) for p in range(4))
        merged_ref[core if n == 0 else 1 - core] = total
    chunk = lax.broadcasted_iota(jnp.int32, (MERGE_PAD, 128), 1) // 32
    for tile in range(4):
        for c in range(2):
            parts = [
                merged_ref[c, lev * MERGE_PAD : (lev + 1) * MERGE_PAD, tile * 128 : (tile + 1) * 128] for lev in range(4)
            ]
            for d in range(4):
                value = jnp.zeros((MERGE_PAD, 128), F32)
                for lev in range(4):
                    shift = (lev - d) % 4 * 32
                    moved = pltpu.roll(parts[lev], shift, 1) if shift else parts[lev]
                    value = jnp.where(chunk == lev, moved, value)
                message_ref[tile * 4 + d, c * 36 : c * 36 + 36, :] = value[:36]
    for block in range(16):
        z, y = block // 2, block % 2
        out_ref[y * 8 + z] = message_ref[block].astype(BF)


def unpack_kernel(in_ref, out_ref, rows_ref):
    for n in range(16):
        rows_ref[n * 72 : (n + 1) * 72, :] = in_ref[n].astype(F32)
    for a in range(6):
        piece = rows_ref[pl.ds(a, 192, stride=6), :]
        out_ref[a] = pltpu.roll(piece, 3, 0).T.astype(BF)


VMEM = pl.BlockSpec(memory_space=pltpu.VMEM)
ANY = pl.BlockSpec(memory_space=pl.ANY)


def call(kernel, out_shape, in_specs, scratch, flops, limit, name):
    out_specs = jax.tree.map(lambda _: VMEM, out_shape)
    return pl.pallas_call(
        kernel,
        out_shape=out_shape,
        in_specs=in_specs,
        out_specs=out_specs,
        scratch_shapes=scratch,
        compiler_params=pltpu.CompilerParams(vmem_limit_bytes=limit),
        cost_estimate=pl.CostEstimate(flops=flops, bytes_accessed=8 << 20, transcendentals=0),
        name=name,
    )


def weight_scratch():
    return [
        pltpu.VMEM((WIDTH, 2 * WIDTH), BF),
        pltpu.VMEM((WIDTH, WIDTH), BF),
        pltpu.VMEM((HEADS, WIN, WIN), F32),
        pltpu.VMEM((WIDTH, WIDTH), BF),
        pltpu.VMEM((WIDTH, FFN), BF),
        pltpu.VMEM((FFN, WIDTH), BF),
    ]


def on_device(tokens, norm_attn, w_qkv, pos_bias, w_out, norm_mlp, w_up, w_down, norm_merge, w_merge):
    shape = lambda s, d=BF: jax.ShapeDtypeStruct(s, d)
    lat_count = lax.axis_size("lat")
    lon_count = lax.axis_size("lon")
    chips = lon_count // 2
    half = lon_count // 2
    zs = chips // 2

    right_own = tokens[:, :HALF].reshape(BAND, WIDTH)
    left = tokens[:, HALF:].reshape(BAND, WIDTH)
    right = lax.ppermute(right_own, "lon", [((i + 1) % lon_count, i) for i in range(lon_count)])

    w_own = w_merge.T
    w_pair = lax.ppermute(w_own, "lon", [(i, (i + half) % lon_count) for i in range(lon_count)])
    first = lax.axis_index("lon") < half
    w_two = jnp.concatenate([jnp.where(first, w_own, w_pair), jnp.where(first, w_pair, w_own)], axis=0)
    rings = [[y * half + 2 * z + c for z in range(zs)] for y in range(2) for c in range(2)]
    w_cols = lax.all_gather(w_two, "lon", axis=0, tiled=True, axis_index_groups=rings)

    bias_perm = jnp.asarray(bias_permutation(), BF)
    eye = jnp.asarray(np.eye(WIDTH, dtype=np.float32), BF)
    bias, wvt = call(
        prepare_kernel, (shape((HEADS, WIN, WIN), F32), shape((WIDTH, WIDTH))), [VMEM] * 4, [], 4 * 10**9, 24 << 20, "prepare"
    )(pos_bias, w_qkv, bias_perm, eye)

    top_rows = jnp.stack([left[:HALF_WIN], right[:HALF_WIN]])
    bottom_rows = jnp.stack([left[-HALF_WIN:], right[-HALF_WIN:]])
    from_above = lax.ppermute(bottom_rows, "lat", [(i, i + 1) for i in range(lat_count - 1)])
    from_below = lax.ppermute(top_rows, "lat", [(i + 1, i) for i in range(lat_count - 1)])

    band = band_permutation()
    middle = np.zeros((2, BAND, BAND), np.float32)
    for n in range(2):
        middle[n, :, 72:216] = band[:, n * 144 : (n + 1) * 144]
    edges = np.stack([band[:, n * 72 : (n + 1) * 72] for n in range(4)])
    eye_win = jnp.asarray(np.eye(WIN, dtype=np.float32), BF)
    eye_half = jnp.asarray(np.eye(HALF_WIN, dtype=np.float32), BF)
    ga, gm = norm_attn.reshape(1, WIDTH), norm_mlp.reshape(1, WIDTH)
    weights = (w_qkv, wvt, bias, w_out, w_up, w_down)

    block1 = call(
        middle_kernel,
        shape((BAND, WIDTH)),
        [VMEM] * 6 + [ANY] * 6,
        weight_scratch()
        + [pltpu.VMEM((2, WIDTH, WIN), BF), pltpu.VMEM((2, WIDTH, WIN), BF), pltpu.SemaphoreType.DMA((6,))],
        9 * 10**9,
        40 << 20,
        "middle",
    )(left, right, jnp.asarray(middle, BF), eye_win, ga, gm, *weights)

    s1, s2 = merge_permutation()
    joined = call(
        edge_kernel,
        shape((4, 4 * MERGE_PAD, WIDTH)),
        [VMEM] * 14 + [ANY] * 6,
        weight_scratch()
        + [pltpu.VMEM((4, WIDTH, WIN), BF), pltpu.VMEM((4, WIDTH, HALF_WIN), BF), pltpu.SemaphoreType.DMA((6,))],
        10 * 10**9,
        40 << 20,
        "edges",
    )(
        top_rows[0], top_rows[1], bottom_rows[0], bottom_rows[1], from_above, from_below, block1, jnp.asarray(edges, BF),
        eye_half, ga, gm, norm_merge.reshape(4, 1, WIDTH), jnp.asarray(s1, BF), jnp.asarray(s2, BF), *weights,
    )

    neighbour = lax.ppermute(joined, "lon", [(i, i ^ 1) for i in range(lon_count)])
    messages = call(
        merge_kernel,
        shape((16, 72, 128)),
        [VMEM] * 3,
        [pltpu.VMEM((2, 4 * MERGE_PAD, WIDTH), F32), pltpu.VMEM((16, 72, 128), F32)],
        10**9,
        32 << 20,
        "merge",
    )(joined, neighbour, w_cols)
    cores = [[2 * i + c for i in range(chips)] for c in range(2)]
    received = lax.all_to_all(messages, "lon", 0, 0, tiled=True, axis_index_groups=cores)
    out = call(
        unpack_kernel, shape((6, 128, 192)), [VMEM], [pltpu.VMEM((1152, 128), F32)], 10**8, 16 << 20, "unpack"
    )(received)
    return out.reshape(6, 4, 32, 192).transpose(0, 3, 1, 2)


def solution(mesh):
    in_specs = (P("lat", "lon", None, None), P(), P(), P(), P(), P(), P(), P(), P(), P(None, "lon"))
    out_specs = P("lat", None, None, "lon")
    return jax.shard_map(on_device, mesh=mesh, in_specs=in_specs, out_specs=out_specs, check_vma=False)
```

```python
import jax
import jax.numpy as jnp
from jax import lax
from jax.experimental import pallas as pl
from jax.experimental.pallas import tpu as pltpu
from jax.sharding import PartitionSpec as P

HEADS = 16
HEAD_DIM = 32
WIDTH = 512
FFN = 2048
ROWS = 12
HALF = 6
WIN = 144
HALF_WIN = 72
BAND = 288
LOG2E = 1.4426950408889634
EPS = 1e-05
BIG = -1e30
BF = jnp.bfloat16
F32 = jnp.float32
LEVELS = ((1, 2), (3, 0))
MERGE_PAD = 40
Z_STEPS = (0, -1, -2, -3, 1, 2, 3, 4)


def dot(a, b, dims=((1,), (0,))):
    return lax.dot_general(a, b, (dims, ((), ())), preferred_element_type=F32)


NT = ((1,), (1,))


def count_steps(value, starts):
    return sum((value >= start).astype(jnp.int32) for start in starts)


def one_hot(column, width):
    lane = lax.broadcasted_iota(jnp.int32, (column.shape[0], width), 1)
    return jnp.where(lane == column, 1.0, 0.0).astype(BF)


def row_numbers(count):
    return lax.broadcasted_iota(jnp.int32, (count, 1), 0)


def split_window(n):
    ihalf = count_steps(n, (72,))
    k = count_steps(n - 72 * ihalf, (36,))
    rest = n - 72 * ihalf - 36 * k
    i3 = count_steps(rest, (12, 24))
    return ihalf, k, i3, rest - 12 * i3


def bias_permutation():
    ihalf, k, i3, j = split_window(row_numbers(WIN))
    return one_hot(2 * (36 * ihalf + 12 * i3 + j) + k, WIN)


def band_places():
    n = row_numbers(BAND)
    t = count_steps(n, (WIN,))
    ihalf, k, i3, j = split_window(n - WIN * t)
    half = count_steps(j, (6,))
    level = jnp.where(t == 0, 1 + k, 3 - 3 * k)
    return half, ihalf, 24 * i3 + 4 * (j - 6 * half) + level


def merge_places(dj, di):
    n = row_numbers(4 * MERGE_PAD)
    level = count_steps(n, (MERGE_PAD, 2 * MERGE_PAD, 3 * MERGE_PAD))
    q = n - MERGE_PAD * level
    b = count_steps(q, (6, 12, 18, 24, 30))
    r, j = 2 * (q - 6 * b) + di, 2 * b + dj
    t = jnp.where((level == 0) | (level == 3), 1, 0)
    k = jnp.where((level == 0) | (level == 2), 1, 0)
    place = 36 * k + j
    ihalf = count_steps(r, (6,))
    band = count_steps(r, (9,))
    middle = 144 * t + 72 * ihalf + 12 * (r - 3 - 3 * ihalf) + place
    edge = 72 * (2 * band + t) + 12 * (r - 9 * band) + place
    inside = (r >= 3) & (r < 9)
    real = q < 36
    return jnp.where(real & inside, middle, -1), jnp.where(real & ~inside, edge, -1)


def normalise(x, gain):
    mean = jnp.sum(x, axis=-1, keepdims=True) * (1.0 / WIDTH)
    centred = x - mean
    spread = jnp.sum(centred * centred, axis=-1, keepdims=True) * (1.0 / WIDTH)
    return centred * lax.rsqrt(spread + EPS) * gain


def split3(x):
    hi = x.astype(BF)
    rest = x - hi.astype(F32)
    mid = rest.astype(BF)
    return hi, mid, (rest - mid.astype(F32)).astype(BF)


def split_kernel(tokens_hbm, right_out, left_out, right_ref, left_ref, sems):
    parts = ((right_ref, 0, right_out), (left_ref, HALF, left_out))
    copies = []
    for n, (held, start, _) in enumerate(parts):
        copies.append(pltpu.make_async_copy(tokens_hbm.at[:, start : start + HALF], held, sems.at[n]))
        copies[-1].start()
    for copy, (held, _, out) in zip(copies, parts):
        copy.wait()
        out[...] = held[...].astype(F32).reshape(BAND, WIDTH).astype(BF)


def prepare_kernel(bias_ref, middle_out, edges_out):
    perm = bias_permutation()
    for h in range(HEADS):
        b = bias_ref[h] * LOG2E
        y = sum(dot(perm, part, NT) for part in split3(b))
        t = sum(dot(part, perm, NT) for part in split3(y))
        tile, n = h // 4, h % 4
        middle_out[tile, :, n * WIN : (n + 1) * WIN] = t
        for half in range(2):
            edges_out[half, tile, :, n * HALF_WIN : (n + 1) * HALF_WIN] = t[:, half * HALF_WIN : (half + 1) * HALF_WIN]


def attend_window(normed, q, k, bias, kaug, qaug, wvt):
    count = q.shape[0]
    k = k.astype(BF)
    vt = dot(wvt, normed, NT).astype(BF)
    lane = lax.broadcasted_iota(jnp.int32, (count, 128), 1) // HEAD_DIM
    scores = []
    for tile in range(4):
        lanes = slice(tile * 128, tile * 128 + 128)
        part = q[:, lanes]
        qm = jnp.concatenate([jnp.where(lane == n, part, 0.0) for n in range(4)], axis=0).astype(BF)
        kx = jnp.concatenate([k[:, lanes], kaug], axis=1)
        qx = jnp.concatenate([qm, qaug], axis=1)
        scores.append(dot(kx, qx, NT) + bias(tile))
    row_head = lax.broadcasted_iota(jnp.int32, (128, 4 * count), 0) // HEAD_DIM
    column = lax.broadcasted_iota(jnp.int32, (128, 4 * count), 1)
    column_head = sum((column >= n * count).astype(jnp.int32) for n in range(1, 4))
    own = row_head == column_head
    pick_row = lax.broadcasted_iota(jnp.int32, (count, 4 * count), 0)
    pick_column = lax.broadcasted_iota(jnp.int32, (count, 4 * count), 1)
    pick = sum((pick_column == pick_row + n * count).astype(F32) for n in range(4)).astype(BF)
    mixed = []
    for tile in range(4):
        s = scores[tile]
        p = jnp.exp2(s - jnp.max(s, axis=0, keepdims=True))
        inverse = 1.0 / jnp.sum(p, axis=0, keepdims=True)
        o = dot(vt[tile * 128 : tile * 128 + 128], p.astype(BF))
        mixed.append(dot(pick, jnp.where(own, o * inverse, 0.0).astype(BF), NT))
    return jnp.concatenate(mixed, axis=1)


def feed_forward(attended, norm_mlp, up_ref, down_ref):
    normed = normalise(attended, norm_mlp).astype(BF)
    acc = attended
    step = 512
    for c in range(0, FFN, step):
        h = dot(normed, up_ref[:, c : c + step])
        h = 0.5 * h * (1.0 + lax.erf(h * 0.7071067811865476))
        acc = acc + dot(h.astype(BF), down_ref[c : c + step, :])
    return acc


def group_lanes(count):
    row = lax.broadcasted_iota(jnp.int32, (count, 128), 0)
    lane = lax.broadcasted_iota(jnp.int32, (count, 128), 1)
    return (row % HALF_WIN) // 36, row // HALF_WIN, lane


def query_key(x, gain, wqkv_ref):
    normed = normalise(x, gain).astype(BF)
    qk = dot(normed, wqkv_ref[:, : 2 * WIDTH])
    return normed, qk[:, :WIDTH] * (LOG2E * HEAD_DIM**-0.5), qk[:, WIDTH:]


def middle_attention_kernel(left_ref, right_ref, ga_ref, wqkv_ref, bias_ref, wout_ref, out_ref, wvt_ref):
    half, ihalf, place = band_places()
    place = 72 + 72 * ihalf + place
    x = dot(one_hot(jnp.where(half == 0, place, -1), BAND), left_ref[...])
    x = x + dot(one_hot(jnp.where(half == 1, place, -1), BAND), right_ref[...])
    normed, q, k = query_key(x, ga_ref[...], wqkv_ref)
    group, _, lane = group_lanes(WIN)
    qgroup, _, qlane = group_lanes(4 * WIN)
    qaug = jnp.where(qlane == qgroup, 1.0, 0.0).astype(BF)
    wvt = dot(one_hot(row_numbers(WIDTH), WIDTH), wqkv_ref[:, 2 * WIDTH :], NT).astype(BF)
    wvt_ref[...] = wvt
    pieces = []
    for t in range(2):
        rows = slice(t * WIN, (t + 1) * WIN)
        kaug = jnp.where((lane < 2) & (lane != group), BIG if t else 0.0, 0.0).astype(BF)
        pieces.append(attend_window(normed[rows], q[rows], k[rows], lambda n: bias_ref[n], kaug, qaug, wvt))
    update = dot(jnp.concatenate(pieces, axis=0).astype(BF), wout_ref[...])
    out_ref[...] = (x + update).astype(BF)


def middle_mlp_kernel(x_ref, gm_ref, up_ref, down_ref, out_ref):
    out_ref[...] = feed_forward(x_ref[...].astype(F32), gm_ref[...], up_ref, down_ref).astype(BF)


def edge_attention_kernel(
    lt_ref, rt_ref, lb_ref, rb_ref, top_ref, bottom_ref, ga_ref, wqkv_ref, wvt_ref, bias_ref, wout_ref, out_ref
):
    bands = (
        (top_ref[0], lt_ref[...], top_ref[1], rt_ref[...]),
        (lb_ref[...], bottom_ref[0], rb_ref[...], bottom_ref[1]),
    )
    half, ihalf, place = band_places()
    perm = [one_hot(jnp.where(2 * half + ihalf == n, place, -1), HALF_WIN) for n in range(4)]
    x = jnp.concatenate([sum(dot(perm[n], piece) for n, piece in enumerate(band)) for band in bands], axis=0)
    normed, q, k = query_key(x, ga_ref[...], wqkv_ref)
    group, half, lane = group_lanes(WIN)
    qgroup, _, qlane = group_lanes(4 * HALF_WIN)
    qaug = jnp.where(qlane == qgroup, 1.0, 0.0).astype(BF)
    lat = lax.axis_index("lat")
    wvt = wvt_ref[...]
    pieces = []
    kept = []
    for n in range(2):
        outside = half == n
        off = jnp.where(lat == (lax.axis_size("lat") - 1 if n else 0), BIG, 0.0)
        for t in range(2):
            first = (n * 2 + t) * WIN
            rows = slice(first, first + WIN)
            queries = slice(first, first + HALF_WIN) if n else slice(first + HALF_WIN, first + WIN)
            other = jnp.where(lane != group, BIG if t else 0.0, 0.0)
            kaug = jnp.where(lane < 2, jnp.where(outside, jnp.minimum(off, other), other), 0.0).astype(BF)
            pieces.append(
                attend_window(normed[rows], q[queries], k[rows], lambda m: bias_ref[1 - n, m], kaug, qaug, wvt)
            )
            kept.append(x[queries])
    update = dot(jnp.concatenate(pieces, axis=0).astype(BF), wout_ref[...])
    out_ref[...] = (jnp.concatenate(kept, axis=0) + update).astype(BF)


def edge_mlp_kernel(x_ref, blk1_ref, gm_ref, up_ref, down_ref, gg_ref, out_ref):
    block = feed_forward(x_ref[...].astype(F32), gm_ref[...], up_ref, down_ref).astype(BF)
    first = blk1_ref[...]
    patches = []
    for p in range(4):
        middle, edge = merge_places(p // 2, p % 2)
        patches.append(dot(one_hot(middle, BAND), first) + dot(one_hot(edge, BAND), block))
    mean = sum(jnp.sum(v, axis=-1, keepdims=True) for v in patches) * (1.0 / (4 * WIDTH))
    centred = [v - mean for v in patches]
    spread = sum(jnp.sum(v * v, axis=-1, keepdims=True) for v in centred) * (1.0 / (4 * WIDTH))
    scale = lax.rsqrt(spread + EPS)
    for p in range(4):
        out_ref[p] = (centred[p] * scale * gg_ref[p]).astype(BF)


def merge_columns(joined_ref, w_refs):
    total = 0.0
    for p in range(4):
        lanes = slice(p * WIDTH, (p + 1) * WIDTH)
        w = jnp.concatenate([r[:, lanes] for r in w_refs], axis=0)
        total = total + dot(joined_ref[p], w, NT)
    return total


def merge_own_kernel(joined_ref, *refs):
    w_refs, out_ref = refs[:-1], refs[-1]
    out_ref[:, :256] = merge_columns(joined_ref, w_refs[:5])
    out_ref[:, 256:] = merge_columns(joined_ref, w_refs[5:])


def merge_kernel(joined_ref, own_ref, *refs):
    w_refs, (out_ref, merged_ref, message_ref) = refs[:-3], refs[-3:]
    lon = lax.axis_index("lon")
    chips = lax.axis_size("lon") // 2
    core = lax.rem(lon, 2)
    z = lax.rem(lon // 2, 8)
    y = lon // chips
    merged_ref[core] = own_ref[...]
    merged_ref[1 - core, :, :256] = merge_columns(joined_ref, w_refs[:5])
    merged_ref[1 - core, :, 256:] = merge_columns(joined_ref, w_refs[5:])
    chunk = lax.broadcasted_iota(jnp.int32, (MERGE_PAD, 128), 1) // 32
    for tile in range(4):
        for c in range(2):
            parts = [
                merged_ref[c, lev * MERGE_PAD : (lev + 1) * MERGE_PAD, tile * 128 : (tile + 1) * 128] for lev in range(4)
            ]
            for d in range(4):
                value = jnp.zeros((MERGE_PAD, 128), F32)
                for lev in range(4):
                    shift = (lev - d) % 4 * 32
                    moved = pltpu.roll(parts[lev], shift, 1) if shift else parts[lev]
                    value = jnp.where(chunk == lev, moved, value)
                message_ref[tile * 4 + d, c * 36 : c * 36 + 36, :] = value[:36]
    for block in range(16):
        zd = lax.rem(z + Z_STEPS[block // 2] + 8, 8)
        yd = 1 - y if block % 2 else y
        out_ref[yd * 8 + zd] = message_ref[block].astype(BF)


def unpack_kernel(in_ref, out_ref, rows_ref):
    for n in range(16):
        rows_ref[n * 72 : (n + 1) * 72, :] = in_ref[n].astype(F32)
    for a in range(6):
        piece = rows_ref[pl.ds(a, 192, stride=6), :]
        out_ref[a] = pltpu.roll(piece, 3, 0).T.astype(BF)


VMEM = pl.BlockSpec(memory_space=pltpu.VMEM)
ANY = pl.BlockSpec(memory_space=pl.ANY)


def call(kernel, out_shape, in_specs, scratch, name, limit=28):
    out_specs = jax.tree.map(lambda _: VMEM, out_shape)
    return pl.pallas_call(
        kernel,
        out_shape=out_shape,
        in_specs=in_specs,
        out_specs=out_specs,
        scratch_shapes=scratch,
        compiler_params=pltpu.CompilerParams(vmem_limit_bytes=limit << 20),
        cost_estimate=pl.CostEstimate(flops=1 << 20, bytes_accessed=1 << 16, transcendentals=0),
        name=name,
    )


def on_device(tokens, norm_attn, w_qkv, pos_bias, w_out, norm_mlp, w_up, w_down, norm_merge, w_merge):
    shape = lambda s, d=BF: jax.ShapeDtypeStruct(s, d)
    barrier = lax.optimization_barrier
    lat_count = lax.axis_size("lat")
    lon_count = lax.axis_size("lon")
    chips = lon_count // 2
    held = pltpu.VMEM((ROWS, HALF, 4, WIDTH), BF)

    def around(block, step):
        route = []
        for i in range(lon_count):
            y, z, c = i // chips, i // 2 % 8, i % 2
            route.append((i, y * chips + (z + step) % 8 * 2 + c))
        return lax.ppermute(block, "lon", route)

    w_own = w_merge.T
    w_pair = lax.ppermute(w_own, "lon", [(i, (i + chips) % lon_count) for i in range(lon_count)])
    right_own, left = call(
        split_kernel, (shape((BAND, WIDTH)),) * 2, [ANY], [held, held, pltpu.SemaphoreType.DMA((2,))], "split", 28
    )(tokens)
    right = lax.ppermute(right_own, "lon", [((i + 1) % lon_count, i) for i in range(lon_count)])
    own_up, own_down = around(w_own, 1), around(w_own, -1)
    bias_middle, bias_edges = call(
        prepare_kernel,
        (shape((4, WIN, 4 * WIN), F32), shape((2, 4, WIN, 4 * HALF_WIN), F32)),
        [VMEM],
        [],
        "prepare",
    )(pos_bias)
    bias_middle, w_pair = barrier((bias_middle, w_pair))
    pair_up, pair_down = around(w_pair, 1), around(w_pair, -1)

    top_rows = jnp.stack([left[:HALF_WIN], right[:HALF_WIN]])
    bottom_rows = jnp.stack([left[-HALF_WIN:], right[-HALF_WIN:]])
    from_above = lax.ppermute(bottom_rows, "lat", [(i, i + 1) for i in range(lat_count - 1)])
    top_rows, own_up, own_down, pair_up, pair_down = barrier((top_rows, own_up, own_down, pair_up, pair_down))
    up, down = [jnp.concatenate([own_up, pair_up], axis=0)], [jnp.concatenate([own_down, pair_down], axis=0)]
    up.append(around(up[-1], 1))
    down.append(around(down[-1], -1))
    from_below = lax.ppermute(top_rows, "lat", [(i + 1, i) for i in range(lat_count - 1)])

    ga, gm = norm_attn.reshape(1, WIDTH), norm_mlp.reshape(1, WIDTH)
    attended1, wvt = call(
        middle_attention_kernel, (shape((BAND, WIDTH)), shape((WIDTH, WIDTH))), [VMEM] * 6, [], "middle_attention"
    )(left, right, ga, w_qkv, bias_middle, w_out)
    attended1, wvt, from_above, u, d = barrier((attended1, wvt, from_above, up[-1], down[-1]))
    up.append(around(u, 1))
    down.append(around(d, -1))
    block1 = call(middle_mlp_kernel, shape((BAND, WIDTH)), [VMEM] * 4, [], "middle_mlp")(attended1, gm, w_up, w_down)
    attended2 = call(edge_attention_kernel, shape((BAND, WIDTH)), [VMEM] * 11, [], "edge_attention")(
        top_rows[0], top_rows[1], bottom_rows[0], bottom_rows[1], from_above, from_below, ga, w_qkv, wvt, bias_edges, w_out
    )
    attended2, block1, u, d = barrier((attended2, block1, up[-1], down[-1]))
    far_up, far_down = around(u[:32], 1), around(d[32:], -1)
    joined = call(edge_mlp_kernel, shape((4, 4 * MERGE_PAD, WIDTH)), [VMEM] * 6, [], "edge_mlp")(
        attended2, block1, gm, w_up, w_down, norm_merge.reshape(4, 1, WIDTH)
    )
    joined, far_up, far_down = barrier((joined, far_up, far_down))
    neighbour = lax.ppermute(joined, "lon", [(i, i ^ 1) for i in range(lon_count)])
    w_cols = [w_own, w_pair] + up + down + [far_up, far_down]
    own = call(merge_own_kernel, shape((4 * MERGE_PAD, WIDTH), F32), [VMEM] * 11, [], "merge_own")(joined, *w_cols)
    messages = call(
        merge_kernel,
        shape((16, 72, 128)),
        [VMEM] * 12,
        [pltpu.VMEM((2, 4 * MERGE_PAD, WIDTH), F32), pltpu.VMEM((16, 72, 128), F32)],
        "merge",
    )(neighbour, own, *w_cols)
    cores = [[2 * i + c for i in range(chips)] for c in range(2)]
    received = lax.all_to_all(messages, "lon", 0, 0, tiled=True, axis_index_groups=cores)
    out = call(unpack_kernel, shape((6, 128, 192)), [VMEM], [pltpu.VMEM((1152, 128), F32)],  "unpack")(received)
    return out.reshape(6, 4, 32, 192).transpose(0, 3, 1, 2)


def solution(mesh):
    in_specs = (P("lat", "lon", None, None), P(), P(), P(), P(), P(), P(), P(), P(), P(None, "lon"))
    out_specs = P("lat", None, None, "lon")
    return jax.shard_map(on_device, mesh=mesh, in_specs=in_specs, out_specs=out_specs, check_vma=False)
```

```python
import jax
import jax.numpy as jnp
from jax import lax
from jax.experimental import pallas as pl
from jax.experimental.pallas import tpu as pltpu
from jax.sharding import PartitionSpec as P

HEADS = 16
HEAD_DIM = 32
WIDTH = 512
FFN = 2048
ROWS = 12
HALF = 6
WIN = 144
HALF_WIN = 72
BAND = 288
LOG2E = 1.4426950408889634
EPS = 1e-05
BIG = -1e30
BF = jnp.bfloat16
F32 = jnp.float32
LEVELS = ((1, 2), (3, 0))
MERGE_PAD = 40
Z_STEPS = (0, -1, -2, -3, 1, 2, 3, 4)


def dot(a, b, dims=((1,), (0,))):
    return lax.dot_general(a, b, (dims, ((), ())), preferred_element_type=F32)


NT = ((1,), (1,))


def count_steps(value, starts):
    return sum((value >= start).astype(jnp.int32) for start in starts)


def one_hot(column, width):
    lane = lax.broadcasted_iota(jnp.int32, (column.shape[0], width), 1)
    return jnp.where(lane == column, 1.0, 0.0).astype(BF)


def row_numbers(count):
    return lax.broadcasted_iota(jnp.int32, (count, 1), 0)


def split_window(n):
    ihalf = count_steps(n, (72,))
    k = count_steps(n - 72 * ihalf, (36,))
    rest = n - 72 * ihalf - 36 * k
    i3 = count_steps(rest, (12, 24))
    return ihalf, k, i3, rest - 12 * i3


def bias_permutation():
    ihalf, k, i3, j = split_window(row_numbers(WIN))
    return one_hot(2 * (36 * ihalf + 12 * i3 + j) + k, WIN)


def band_places():
    n = row_numbers(BAND)
    t = count_steps(n, (WIN,))
    ihalf, k, i3, j = split_window(n - WIN * t)
    half = count_steps(j, (6,))
    level = jnp.where(t == 0, 1 + k, 3 - 3 * k)
    return half, ihalf, 24 * i3 + 4 * (j - 6 * half) + level


def merge_places(dj, di):
    n = row_numbers(4 * MERGE_PAD)
    level = count_steps(n, (MERGE_PAD, 2 * MERGE_PAD, 3 * MERGE_PAD))
    q = n - MERGE_PAD * level
    b = count_steps(q, (6, 12, 18, 24, 30))
    r, j = 2 * (q - 6 * b) + di, 2 * b + dj
    t = jnp.where((level == 0) | (level == 3), 1, 0)
    k = jnp.where((level == 0) | (level == 2), 1, 0)
    place = 36 * k + j
    ihalf = count_steps(r, (6,))
    band = count_steps(r, (9,))
    middle = 144 * t + 72 * ihalf + 12 * (r - 3 - 3 * ihalf) + place
    edge = 72 * (2 * band + t) + 12 * (r - 9 * band) + place
    inside = (r >= 3) & (r < 9)
    real = q < 36
    return jnp.where(real & inside, middle, -1), jnp.where(real & ~inside, edge, -1)


def normalise(x, gain):
    mean = jnp.sum(x, axis=-1, keepdims=True) * (1.0 / WIDTH)
    centred = x - mean
    spread = jnp.sum(centred * centred, axis=-1, keepdims=True) * (1.0 / WIDTH)
    return centred * lax.rsqrt(spread + EPS) * gain


def split3(x):
    hi = x.astype(BF)
    rest = x - hi.astype(F32)
    mid = rest.astype(BF)
    return hi, mid, (rest - mid.astype(F32)).astype(BF)


def split_kernel(tokens_hbm, right_out, left_out, right_ref, left_ref, sems):
    parts = ((right_ref, 0, right_out), (left_ref, HALF, left_out))
    copies = []
    for n, (held, start, _) in enumerate(parts):
        copies.append(pltpu.make_async_copy(tokens_hbm.at[:, start : start + HALF], held, sems.at[n]))
        copies[-1].start()
    for copy, (held, _, out) in zip(copies, parts):
        copy.wait()
        out[...] = held[...].astype(F32).reshape(BAND, WIDTH).astype(BF)


def prepare_kernel(bias_ref, out_ref):
    perm = bias_permutation()
    for h in range(HEADS):
        parts = split3(bias_ref[h] * LOG2E)
        out_ref[h] = sum(dot(dot(perm, part).astype(BF), perm, NT) for part in parts)


def attend_window(q, k, v, bias, kaug, qaug):
    count = q.shape[0]
    k, v = k.astype(BF), v.astype(BF)
    lane_head = lax.broadcasted_iota(jnp.int32, (count, 128), 1) // HEAD_DIM
    ones = jnp.ones((WIN, 128), BF)
    mixed = []
    for tile in range(4):
        lanes = slice(tile * 128, tile * 128 + 128)
        part = q[:, lanes]
        qm = jnp.concatenate([jnp.where(lane_head == n, part, 0.0) for n in range(4)], axis=0).astype(BF)
        s = dot(jnp.concatenate([qm, qaug], axis=1), jnp.concatenate([k[:, lanes], kaug], axis=1), NT) + bias(tile)
        p = jnp.exp2(s - jnp.max(s, axis=1, keepdims=True)).astype(BF)
        o = dot(p, jnp.concatenate([v[:, lanes], ones], axis=1))
        o = o[:, :128] * (1.0 / o[:, 128:])
        mixed.append(sum(jnp.where(lane_head == n, o[n * count : (n + 1) * count], 0.0) for n in range(4)))
    return jnp.concatenate(mixed, axis=1).astype(BF)


def feed_forward(attended, norm_mlp, up_ref, down_ref):
    normed = normalise(attended, norm_mlp).astype(BF)
    acc = attended
    step = 512
    for c in range(0, FFN, step):
        h = dot(normed, up_ref[:, c : c + step])
        h = 0.5 * h * (1.0 + lax.erf(h * 0.7071067811865476))
        acc = acc + dot(h.astype(BF), down_ref[c : c + step, :])
    return acc


def group_lanes(count):
    row = lax.broadcasted_iota(jnp.int32, (count, 128), 0)
    lane = lax.broadcasted_iota(jnp.int32, (count, 128), 1)
    return (row % HALF_WIN) // 36, row // HALF_WIN, lane


def middle_attention_kernel(left_ref, right_ref, ga_ref, wqkv_ref, bias_ref, wout_ref, out_ref):
    half, ihalf, place = band_places()
    place = 72 + 72 * ihalf + place
    x = dot(one_hot(jnp.where(half == 0, place, -1), BAND), left_ref[...])
    x = x + dot(one_hot(jnp.where(half == 1, place, -1), BAND), right_ref[...])
    qkv = dot(normalise(x, ga_ref[...]).astype(BF), wqkv_ref[...])
    q = qkv[:, :WIDTH] * (LOG2E * HEAD_DIM**-0.5)
    group, _, lane = group_lanes(WIN)
    qgroup, _, qlane = group_lanes(4 * WIN)
    qaug = jnp.where(qlane == qgroup, 1.0, 0.0).astype(BF)

    def bias(tile):
        return jnp.concatenate([bias_ref[4 * tile + n] for n in range(4)], axis=0)

    pieces = []
    for t in range(2):
        rows = slice(t * WIN, (t + 1) * WIN)
        kaug = jnp.where((lane < 2) & (lane != group), BIG if t else 0.0, 0.0).astype(BF)
        pieces.append(attend_window(q[rows], qkv[rows, WIDTH : 2 * WIDTH], qkv[rows, 2 * WIDTH :], bias, kaug, qaug))
    update = dot(jnp.concatenate(pieces, axis=0), wout_ref[...])
    out_ref[...] = (x + update).astype(BF)


def middle_mlp_kernel(x_ref, gm_ref, up_ref, down_ref, out_ref):
    out_ref[...] = feed_forward(x_ref[...].astype(F32), gm_ref[...], up_ref, down_ref).astype(BF)


def edge_attention_kernel(
    lt_ref, rt_ref, lb_ref, rb_ref, top_ref, bottom_ref, ga_ref, wqkv_ref, bias_ref, wout_ref, out_ref
):
    bands = (
        (top_ref[0], lt_ref[...], top_ref[1], rt_ref[...]),
        (lb_ref[...], bottom_ref[0], rb_ref[...], bottom_ref[1]),
    )
    half, ihalf, place = band_places()
    perm = [one_hot(jnp.where(2 * half + ihalf == n, place, -1), HALF_WIN) for n in range(4)]
    x = jnp.concatenate([sum(dot(perm[n], piece) for n, piece in enumerate(band)) for band in bands], axis=0)
    normed = normalise(x, ga_ref[...])
    kv = dot(normed.astype(BF), wqkv_ref[:, WIDTH:])
    group, half, lane = group_lanes(WIN)
    qgroup, _, qlane = group_lanes(4 * HALF_WIN)
    qaug = jnp.where(qlane == qgroup, 1.0, 0.0).astype(BF)
    lat = lax.axis_index("lat")
    starts = [(n * 2 + t) * WIN + (1 - n) * HALF_WIN for n in range(2) for t in range(2)]
    asked = jnp.concatenate([normed[start : start + HALF_WIN] for start in starts], axis=0).astype(BF)
    q = dot(asked, wqkv_ref[:, :WIDTH]) * (LOG2E * HEAD_DIM**-0.5)
    pieces = []
    for w, start in enumerate(starts):
        n, t = w // 2, w % 2
        off = jnp.where(lat == (lax.axis_size("lat") - 1 if n else 0), BIG, 0.0)
        other = jnp.where(lane != group, BIG if t else 0.0, 0.0)
        kaug = jnp.where(lane < 2, jnp.where(half == n, jnp.minimum(off, other), other), 0.0).astype(BF)
        rows = slice(w * WIN, (w + 1) * WIN)

        def bias(tile):
            asked_rows = slice((1 - n) * HALF_WIN, (2 - n) * HALF_WIN)
            return jnp.concatenate([bias_ref[4 * tile + m, asked_rows, :] for m in range(4)], axis=0)

        mixed = attend_window(q[w * HALF_WIN : (w + 1) * HALF_WIN], kv[rows, :WIDTH], kv[rows, WIDTH:], bias, kaug, qaug)
        pieces.append(mixed.astype(F32))
    update = dot(jnp.concatenate(pieces, axis=0).astype(BF), wout_ref[...])
    kept = jnp.concatenate([x[start : start + HALF_WIN] for start in starts], axis=0)
    out_ref[...] = (kept + update).astype(BF)


def edge_mlp_kernel(x_ref, blk1_ref, gm_ref, up_ref, down_ref, gg_ref, out_ref):
    block = feed_forward(x_ref[...].astype(F32), gm_ref[...], up_ref, down_ref).astype(BF)
    first = blk1_ref[...]
    patches = []
    for p in range(4):
        middle, edge = merge_places(p // 2, p % 2)
        patches.append(dot(one_hot(middle, BAND), first) + dot(one_hot(edge, BAND), block))
    mean = sum(jnp.sum(v, axis=-1, keepdims=True) for v in patches) * (1.0 / (4 * WIDTH))
    centred = [v - mean for v in patches]
    spread = sum(jnp.sum(v * v, axis=-1, keepdims=True) for v in centred) * (1.0 / (4 * WIDTH))
    scale = lax.rsqrt(spread + EPS)
    for p in range(4):
        out_ref[p] = (centred[p] * scale * gg_ref[p]).astype(BF)


def merge_columns(joined_ref, w_refs):
    total = 0.0
    for p in range(4):
        lanes = slice(p * WIDTH, (p + 1) * WIDTH)
        w = jnp.concatenate([r[:, lanes] for r in w_refs], axis=0)
        total = total + dot(joined_ref[p], w, NT)
    return total


def merge_own_kernel(joined_ref, *refs):
    w_refs, out_ref = refs[:-1], refs[-1]
    out_ref[:, :256] = merge_columns(joined_ref, w_refs[:5])
    out_ref[:, 256:] = merge_columns(joined_ref, w_refs[5:])


def merge_kernel(joined_ref, own_ref, *refs):
    w_refs, (out_ref, merged_ref, message_ref) = refs[:-3], refs[-3:]
    lon = lax.axis_index("lon")
    chips = lax.axis_size("lon") // 2
    core = lax.rem(lon, 2)
    z = lax.rem(lon // 2, 8)
    y = lon // chips
    merged_ref[core] = own_ref[...]
    merged_ref[1 - core, :, :256] = merge_columns(joined_ref, w_refs[:5])
    merged_ref[1 - core, :, 256:] = merge_columns(joined_ref, w_refs[5:])
    chunk = lax.broadcasted_iota(jnp.int32, (MERGE_PAD, 128), 1) // 32
    for tile in range(4):
        for c in range(2):
            parts = [
                merged_ref[c, lev * MERGE_PAD : (lev + 1) * MERGE_PAD, tile * 128 : (tile + 1) * 128] for lev in range(4)
            ]
            for d in range(4):
                value = jnp.zeros((MERGE_PAD, 128), F32)
                for lev in range(4):
                    shift = (lev - d) % 4 * 32
                    moved = pltpu.roll(parts[lev], shift, 1) if shift else parts[lev]
                    value = jnp.where(chunk == lev, moved, value)
                message_ref[tile * 4 + d, c * 36 : c * 36 + 36, :] = value[:36]
    for block in range(16):
        zd = lax.rem(z + Z_STEPS[block // 2] + 8, 8)
        yd = 1 - y if block % 2 else y
        out_ref[yd * 8 + zd] = message_ref[block].astype(BF)


def unpack_kernel(in_ref, out_ref, rows_ref):
    for n in range(16):
        rows_ref[n * 72 : (n + 1) * 72, :] = in_ref[n].astype(F32)
    for a in range(6):
        piece = rows_ref[pl.ds(a, 192, stride=6), :]
        out_ref[a] = pltpu.roll(piece, 3, 0).T.astype(BF)


VMEM = pl.BlockSpec(memory_space=pltpu.VMEM)
ANY = pl.BlockSpec(memory_space=pl.ANY)


def call(kernel, out_shape, in_specs, scratch, name, limit=28):
    out_specs = jax.tree.map(lambda _: VMEM, out_shape)
    return pl.pallas_call(
        kernel,
        out_shape=out_shape,
        in_specs=in_specs,
        out_specs=out_specs,
        scratch_shapes=scratch,
        compiler_params=pltpu.CompilerParams(vmem_limit_bytes=limit << 20),
        cost_estimate=pl.CostEstimate(flops=1 << 20, bytes_accessed=1 << 16, transcendentals=0),
        name=name,
    )


def on_device(tokens, norm_attn, w_qkv, pos_bias, w_out, norm_mlp, w_up, w_down, norm_merge, w_merge):
    shape = lambda s, d=BF: jax.ShapeDtypeStruct(s, d)
    barrier = lax.optimization_barrier
    lat_count = lax.axis_size("lat")
    lon_count = lax.axis_size("lon")
    chips = lon_count // 2
    held = pltpu.VMEM((ROWS, HALF, 4, WIDTH), BF)

    def around(block, step):
        route = []
        for i in range(lon_count):
            y, z, c = i // chips, i // 2 % 8, i % 2
            route.append((i, y * chips + (z + step) % 8 * 2 + c))
        return lax.ppermute(block, "lon", route)

    w_own = w_merge.T
    w_pair = lax.ppermute(w_own, "lon", [(i, (i + chips) % lon_count) for i in range(lon_count)])
    right_own, left = call(
        split_kernel, (shape((BAND, WIDTH)),) * 2, [ANY], [held, held, pltpu.SemaphoreType.DMA((2,))], "split", 28
    )(tokens)
    right = lax.ppermute(right_own, "lon", [((i + 1) % lon_count, i) for i in range(lon_count)])
    own_up, own_down = around(w_own, 1), around(w_own, -1)
    w_pair, pos_bias = barrier((w_pair, pos_bias))
    pair_up, pair_down = around(w_pair, 1), around(w_pair, -1)
    bias = call(prepare_kernel, shape((HEADS, WIN, WIN), F32), [VMEM], [], "prepare")(pos_bias)

    bias, right, own_up, own_down, pair_up, pair_down = barrier((bias, right, own_up, own_down, pair_up, pair_down))
    up, down = [jnp.concatenate([own_up, pair_up], axis=0)], [jnp.concatenate([own_down, pair_down], axis=0)]
    up.append(around(up[-1], 1))
    down.append(around(down[-1], -1))
    top_rows = jnp.stack([left[:HALF_WIN], right[:HALF_WIN]])
    bottom_rows = jnp.stack([left[-HALF_WIN:], right[-HALF_WIN:]])
    from_above = lax.ppermute(bottom_rows, "lat", [(i, i + 1) for i in range(lat_count - 1)])
    from_below = lax.ppermute(top_rows, "lat", [(i + 1, i) for i in range(lat_count - 1)])
    ga, gm = norm_attn.reshape(1, WIDTH), norm_mlp.reshape(1, WIDTH)
    attended1 = call(middle_attention_kernel, shape((BAND, WIDTH)), [VMEM] * 6, [], "middle_attention")(
        left, right, ga, w_qkv, bias, w_out
    )
    block1 = call(middle_mlp_kernel, shape((BAND, WIDTH)), [VMEM] * 4, [], "middle_mlp")(attended1, gm, w_up, w_down)

    block1, from_above, from_below, u, d = barrier((block1, from_above, from_below, up[-1], down[-1]))
    up.append(around(u, 1))
    down.append(around(d, -1))
    far_up, far_down = around(u[:32], 2), around(d[32:], -2)
    attended2 = call(edge_attention_kernel, shape((BAND, WIDTH)), [VMEM] * 10, [], "edge_attention")(
        top_rows[0], top_rows[1], bottom_rows[0], bottom_rows[1], from_above, from_below, ga, w_qkv, bias, w_out
    )
    joined = call(edge_mlp_kernel, shape((4, 4 * MERGE_PAD, WIDTH)), [VMEM] * 6, [], "edge_mlp")(
        attended2, block1, gm, w_up, w_down, norm_merge.reshape(4, 1, WIDTH)
    )
    joined, far_up, far_down, up[-1], down[-1] = barrier((joined, far_up, far_down, up[-1], down[-1]))
    neighbour = lax.ppermute(joined, "lon", [(i, i ^ 1) for i in range(lon_count)])
    w_cols = [w_own, w_pair] + up + down + [far_up, far_down]
    own = call(merge_own_kernel, shape((4 * MERGE_PAD, WIDTH), F32), [VMEM] * 11, [], "merge_own")(joined, *w_cols)
    messages = call(
        merge_kernel,
        shape((16, 72, 128)),
        [VMEM] * 12,
        [pltpu.VMEM((2, 4 * MERGE_PAD, WIDTH), F32), pltpu.VMEM((16, 72, 128), F32)],
        "merge",
    )(neighbour, own, *w_cols)
    cores = [[2 * i + c for i in range(chips)] for c in range(2)]
    received = lax.all_to_all(messages, "lon", 0, 0, tiled=True, axis_index_groups=cores)
    out = call(unpack_kernel, shape((6, 128, 192)), [VMEM], [pltpu.VMEM((1152, 128), F32)],  "unpack")(received)
    return out.reshape(6, 4, 32, 192).transpose(0, 3, 1, 2)


def solution(mesh):
    in_specs = (P("lat", "lon", None, None), P(), P(), P(), P(), P(), P(), P(), P(), P(None, "lon"))
    out_specs = P("lat", None, None, "lon")
    return jax.shard_map(on_device, mesh=mesh, in_specs=in_specs, out_specs=out_specs, check_vma=False)
```

```python
import jax
import jax.numpy as jnp
from jax import lax
from jax.experimental import pallas as pl
from jax.experimental.pallas import tpu as pltpu
from jax.sharding import PartitionSpec as P

HEADS = 16
HEAD_DIM = 32
WIDTH = 512
FFN = 2048
ROWS = 12
HALF = 6
WIN = 144
HALF_WIN = 72
BAND = 288
LOG2E = 1.4426950408889634
EPS = 1e-05
BIG = -1e30
BF = jnp.bfloat16
F32 = jnp.float32
LEVELS = ((1, 2), (3, 0))
MERGE_PAD = 40
Z_STEPS = (0, -1, -2, -3, 1, 2, 3, 4)


def dot(a, b, dims=((1,), (0,))):
    return lax.dot_general(a, b, (dims, ((), ())), preferred_element_type=F32)


NT = ((1,), (1,))


def count_steps(value, starts):
    return sum((value >= start).astype(jnp.int32) for start in starts)


def one_hot(column, width):
    lane = lax.broadcasted_iota(jnp.int32, (column.shape[0], width), 1)
    return jnp.where(lane == column, 1.0, 0.0).astype(BF)


def row_numbers(count):
    return lax.broadcasted_iota(jnp.int32, (count, 1), 0)


def split_window(n):
    ihalf = count_steps(n, (72,))
    k = count_steps(n - 72 * ihalf, (36,))
    rest = n - 72 * ihalf - 36 * k
    i3 = count_steps(rest, (12, 24))
    return ihalf, k, i3, rest - 12 * i3


def bias_permutation():
    ihalf, k, i3, j = split_window(row_numbers(WIN))
    return one_hot(2 * (36 * ihalf + 12 * i3 + j) + k, WIN)


def band_places():
    n = row_numbers(BAND)
    t = count_steps(n, (WIN,))
    ihalf, k, i3, j = split_window(n - WIN * t)
    half = count_steps(j, (6,))
    level = jnp.where(t == 0, 1 + k, 3 - 3 * k)
    return half, ihalf, 24 * i3 + 4 * (j - 6 * half) + level


def merge_places(dj, di):
    n = row_numbers(4 * MERGE_PAD)
    level = count_steps(n, (MERGE_PAD, 2 * MERGE_PAD, 3 * MERGE_PAD))
    q = n - MERGE_PAD * level
    b = count_steps(q, (6, 12, 18, 24, 30))
    r, j = 2 * (q - 6 * b) + di, 2 * b + dj
    t = jnp.where((level == 0) | (level == 3), 1, 0)
    k = jnp.where((level == 0) | (level == 2), 1, 0)
    place = 36 * k + j
    ihalf = count_steps(r, (6,))
    band = count_steps(r, (9,))
    middle = 144 * t + 72 * ihalf + 12 * (r - 3 - 3 * ihalf) + place
    edge = 72 * (2 * band + t) + 12 * (r - 9 * band) + place
    inside = (r >= 3) & (r < 9)
    real = q < 36
    return jnp.where(real & inside, middle, -1), jnp.where(real & ~inside, edge, -1)


def normalise(x, gain):
    mean = jnp.sum(x, axis=-1, keepdims=True) * (1.0 / WIDTH)
    centred = x - mean
    spread = jnp.sum(centred * centred, axis=-1, keepdims=True) * (1.0 / WIDTH)
    return centred * lax.rsqrt(spread + EPS) * gain


def split3(x):
    hi = x.astype(BF)
    rest = x - hi.astype(F32)
    mid = rest.astype(BF)
    return hi, mid, (rest - mid.astype(F32)).astype(BF)


def split_kernel(tokens_hbm, right_out, left_out, right_ref, left_ref, sems):
    parts = ((right_ref, 0, right_out), (left_ref, HALF, left_out))
    copies = []
    for n, (held, start, _) in enumerate(parts):
        copies.append(pltpu.make_async_copy(tokens_hbm.at[:, start : start + HALF], held, sems.at[n]))
        copies[-1].start()
    for copy, (held, _, out) in zip(copies, parts):
        copy.wait()
        out[...] = held[...].astype(F32).reshape(BAND, WIDTH).astype(BF)


def prepare_kernel(bias_ref, out_ref):
    perm = bias_permutation()
    for h in range(HEADS):
        parts = split3(bias_ref[h] * LOG2E)
        out_ref[h] = sum(dot(dot(perm, part).astype(BF), perm, NT) for part in parts)


def attend_window(q, k, v, bias, kaug, qaug):
    count = q.shape[0]
    k, v = k.astype(BF), v.astype(BF)
    lane_head = lax.broadcasted_iota(jnp.int32, (count, 128), 1) // HEAD_DIM
    ones = jnp.ones((WIN, 128), BF)
    mixed = []
    for tile in range(4):
        lanes = slice(tile * 128, tile * 128 + 128)
        part = q[:, lanes]
        qm = jnp.concatenate([jnp.where(lane_head == n, part, 0.0) for n in range(4)], axis=0).astype(BF)
        s = dot(jnp.concatenate([qm, qaug], axis=1), jnp.concatenate([k[:, lanes], kaug], axis=1), NT) + bias(tile)
        p = jnp.exp2(s - jnp.max(s, axis=1, keepdims=True)).astype(BF)
        o = dot(p, jnp.concatenate([v[:, lanes], ones], axis=1))
        o = o[:, :128] * (1.0 / o[:, 128:])
        mixed.append(sum(jnp.where(lane_head == n, o[n * count : (n + 1) * count], 0.0) for n in range(4)))
    return jnp.concatenate(mixed, axis=1).astype(BF)


def feed_forward(attended, norm_mlp, up_ref, down_ref):
    normed = normalise(attended, norm_mlp).astype(BF)
    acc = attended
    step = 512
    for c in range(0, FFN, step):
        h = dot(normed, up_ref[:, c : c + step])
        h = 0.5 * h * (1.0 + lax.erf(h * 0.7071067811865476))
        acc = acc + dot(h.astype(BF), down_ref[c : c + step, :])
    return acc


def group_lanes(count):
    row = lax.broadcasted_iota(jnp.int32, (count, 128), 0)
    lane = lax.broadcasted_iota(jnp.int32, (count, 128), 1)
    return (row % HALF_WIN) // 36, row // HALF_WIN, lane


def middle_attention_kernel(left_ref, right_ref, ga_ref, wqkv_ref, bias_ref, wout_ref, out_ref):
    half, ihalf, place = band_places()
    place = 72 + 72 * ihalf + place
    x = dot(one_hot(jnp.where(half == 0, place, -1), BAND), left_ref[...])
    x = x + dot(one_hot(jnp.where(half == 1, place, -1), BAND), right_ref[...])
    qkv = dot(normalise(x, ga_ref[...]).astype(BF), wqkv_ref[...])
    q = qkv[:, :WIDTH] * (LOG2E * HEAD_DIM**-0.5)
    group, _, lane = group_lanes(WIN)
    qgroup, _, qlane = group_lanes(4 * WIN)
    qaug = jnp.where(qlane == qgroup, 1.0, 0.0).astype(BF)

    def bias(tile):
        return jnp.concatenate([bias_ref[4 * tile + n] for n in range(4)], axis=0)

    pieces = []
    for t in range(2):
        rows = slice(t * WIN, (t + 1) * WIN)
        kaug = jnp.where((lane < 2) & (lane != group), BIG if t else 0.0, 0.0).astype(BF)
        pieces.append(attend_window(q[rows], qkv[rows, WIDTH : 2 * WIDTH], qkv[rows, 2 * WIDTH :], bias, kaug, qaug))
    update = dot(jnp.concatenate(pieces, axis=0), wout_ref[...])
    out_ref[...] = (x + update).astype(BF)


def middle_mlp_kernel(x_ref, gm_ref, up_ref, down_ref, out_ref):
    out_ref[...] = feed_forward(x_ref[...].astype(F32), gm_ref[...], up_ref, down_ref).astype(BF)


def edge_attention_kernel(
    lt_ref, rt_ref, lb_ref, rb_ref, top_ref, bottom_ref, ga_ref, wqkv_ref, bias_ref, wout_ref, out_ref
):
    bands = (
        (top_ref[0], lt_ref[...], top_ref[1], rt_ref[...]),
        (lb_ref[...], bottom_ref[0], rb_ref[...], bottom_ref[1]),
    )
    half, ihalf, place = band_places()
    perm = [one_hot(jnp.where(2 * half + ihalf == n, place, -1), HALF_WIN) for n in range(4)]
    x = jnp.concatenate([sum(dot(perm[n], piece) for n, piece in enumerate(band)) for band in bands], axis=0)
    normed = normalise(x, ga_ref[...])
    kv = dot(normed.astype(BF), wqkv_ref[:, WIDTH:])
    group, half, lane = group_lanes(WIN)
    qgroup, _, qlane = group_lanes(4 * HALF_WIN)
    qaug = jnp.where(qlane == qgroup, 1.0, 0.0).astype(BF)
    lat = lax.axis_index("lat")
    starts = [(n * 2 + t) * WIN + (1 - n) * HALF_WIN for n in range(2) for t in range(2)]
    asked = jnp.concatenate([normed[start : start + HALF_WIN] for start in starts], axis=0).astype(BF)
    q = dot(asked, wqkv_ref[:, :WIDTH]) * (LOG2E * HEAD_DIM**-0.5)
    pieces = []
    for w, start in enumerate(starts):
        n, t = w // 2, w % 2
        off = jnp.where(lat == (lax.axis_size("lat") - 1 if n else 0), BIG, 0.0)
        other = jnp.where(lane != group, BIG if t else 0.0, 0.0)
        kaug = jnp.where(lane < 2, jnp.where(half == n, jnp.minimum(off, other), other), 0.0).astype(BF)
        rows = slice(w * WIN, (w + 1) * WIN)

        def bias(tile):
            asked_rows = slice((1 - n) * HALF_WIN, (2 - n) * HALF_WIN)
            return jnp.concatenate([bias_ref[4 * tile + m, asked_rows, :] for m in range(4)], axis=0)

        mixed = attend_window(q[w * HALF_WIN : (w + 1) * HALF_WIN], kv[rows, :WIDTH], kv[rows, WIDTH:], bias, kaug, qaug)
        pieces.append(mixed.astype(F32))
    update = dot(jnp.concatenate(pieces, axis=0).astype(BF), wout_ref[...])
    kept = jnp.concatenate([x[start : start + HALF_WIN] for start in starts], axis=0)
    out_ref[...] = (kept + update).astype(BF)


def edge_mlp_kernel(x_ref, blk1_ref, gm_ref, up_ref, down_ref, gg_ref, out_ref):
    block = feed_forward(x_ref[...].astype(F32), gm_ref[...], up_ref, down_ref).astype(BF)
    first = blk1_ref[...]
    patches = []
    for p in range(4):
        middle, edge = merge_places(p // 2, p % 2)
        patches.append(dot(one_hot(middle, BAND), first) + dot(one_hot(edge, BAND), block))
    mean = sum(jnp.sum(v, axis=-1, keepdims=True) for v in patches) * (1.0 / (4 * WIDTH))
    centred = [v - mean for v in patches]
    spread = sum(jnp.sum(v * v, axis=-1, keepdims=True) for v in centred) * (1.0 / (4 * WIDTH))
    scale = lax.rsqrt(spread + EPS)
    for p in range(4):
        out_ref[p] = (centred[p] * scale * gg_ref[p]).astype(BF)


def merge_columns(joined_ref, w_refs):
    chunk = lax.broadcasted_iota(jnp.int32, (MERGE_PAD, 128), 1) // 32
    messages = []
    for part in (w_refs[:5], w_refs[5:]):
        total = 0.0
        for p in range(4):
            lanes = slice(p * WIDTH, (p + 1) * WIDTH)
            total = total + dot(joined_ref[p], jnp.concatenate([r[:, lanes] for r in part], axis=0), NT)
        for tile in range(2):
            levels = [
                total[lev * MERGE_PAD : (lev + 1) * MERGE_PAD, tile * 128 : (tile + 1) * 128] for lev in range(4)
            ]
            for d in range(4):
                value = jnp.zeros((MERGE_PAD, 128), F32)
                for lev in range(4):
                    shift = (lev - d) % 4 * 32
                    moved = pltpu.roll(levels[lev], shift, 1) if shift else levels[lev]
                    value = jnp.where(chunk == lev, moved, value)
                messages.append(value)
    return messages


def merge_own_kernel(joined_ref, *refs):
    for block, value in enumerate(merge_columns(joined_ref, refs[:-1])):
        refs[-1][block] = value


def merge_kernel(joined_ref, own_ref, *refs):
    w_refs, (out_ref, message_ref) = refs[:-2], refs[-2:]
    lon = lax.axis_index("lon")
    chips = lax.axis_size("lon") // 2
    first = lax.rem(lon, 2) == 0
    z = lax.rem(lon // 2, 8)
    y = lon // chips
    for block, other in enumerate(merge_columns(joined_ref, w_refs)):
        own = own_ref[block]
        message_ref[block, :MERGE_PAD] = jnp.where(first, own, other)
        message_ref[block, 36 : 36 + MERGE_PAD] = jnp.where(first, other, own)
        zd = lax.rem(z + Z_STEPS[block // 2] + 8, 8)
        yd = 1 - y if block % 2 else y
        out_ref[yd * 8 + zd] = message_ref[block, :72].astype(BF)


def unpack_kernel(in_ref, out_ref, rows_ref):
    for n in range(16):
        rows_ref[n * 72 : (n + 1) * 72, :] = in_ref[n].astype(F32)
    for a in range(6):
        piece = rows_ref[pl.ds(a, 192, stride=6), :]
        out_ref[a] = pltpu.roll(piece, 3, 0).T.astype(BF)


VMEM = pl.BlockSpec(memory_space=pltpu.VMEM)
ANY = pl.BlockSpec(memory_space=pl.ANY)


def call(kernel, out_shape, in_specs, scratch, name, limit=28):
    out_specs = jax.tree.map(lambda _: VMEM, out_shape)
    return pl.pallas_call(
        kernel,
        out_shape=out_shape,
        in_specs=in_specs,
        out_specs=out_specs,
        scratch_shapes=scratch,
        compiler_params=pltpu.CompilerParams(vmem_limit_bytes=limit << 20),
        cost_estimate=pl.CostEstimate(flops=1 << 20, bytes_accessed=1 << 16, transcendentals=0),
        name=name,
    )


def on_device(tokens, norm_attn, w_qkv, pos_bias, w_out, norm_mlp, w_up, w_down, norm_merge, w_merge):
    shape = lambda s, d=BF: jax.ShapeDtypeStruct(s, d)
    barrier = lax.optimization_barrier
    lat_count = lax.axis_size("lat")
    lon_count = lax.axis_size("lon")
    chips = lon_count // 2
    held = pltpu.VMEM((ROWS, HALF, 4, WIDTH), BF)

    def around(block, step):
        route = []
        for i in range(lon_count):
            y, z, c = i // chips, i // 2 % 8, i % 2
            route.append((i, y * chips + (z + step) % 8 * 2 + c))
        return lax.ppermute(block, "lon", route)

    w_own = w_merge.T
    w_pair = lax.ppermute(w_own, "lon", [(i, (i + chips) % lon_count) for i in range(lon_count)])
    right_own, left = call(
        split_kernel, (shape((BAND, WIDTH)),) * 2, [ANY], [held, held, pltpu.SemaphoreType.DMA((2,))], "split", 28
    )(tokens)
    right = lax.ppermute(right_own, "lon", [((i + 1) % lon_count, i) for i in range(lon_count)])
    own_up, own_down = around(w_own, 1), around(w_own, -1)
    w_pair, pos_bias = barrier((w_pair, pos_bias))
    pair_up, pair_down = around(w_pair, 1), around(w_pair, -1)
    bias = call(prepare_kernel, shape((HEADS, WIN, WIN), F32), [VMEM], [], "prepare")(pos_bias)

    bias, right, own_up, own_down, pair_up, pair_down = barrier((bias, right, own_up, own_down, pair_up, pair_down))
    up, down = [jnp.concatenate([own_up, pair_up], axis=0)], [jnp.concatenate([own_down, pair_down], axis=0)]
    up.append(around(up[-1], 1))
    down.append(around(down[-1], -1))
    top_rows = jnp.stack([left[:HALF_WIN], right[:HALF_WIN]])
    bottom_rows = jnp.stack([left[-HALF_WIN:], right[-HALF_WIN:]])
    from_above = lax.ppermute(bottom_rows, "lat", [(i, i + 1) for i in range(lat_count - 1)])
    from_below = lax.ppermute(top_rows, "lat", [(i + 1, i) for i in range(lat_count - 1)])
    ga, gm = norm_attn.reshape(1, WIDTH), norm_mlp.reshape(1, WIDTH)
    attended1 = call(middle_attention_kernel, shape((BAND, WIDTH)), [VMEM] * 6, [], "middle_attention")(
        left, right, ga, w_qkv, bias, w_out
    )
    block1 = call(middle_mlp_kernel, shape((BAND, WIDTH)), [VMEM] * 4, [], "middle_mlp")(attended1, gm, w_up, w_down)

    block1, from_above, from_below, u, d = barrier((block1, from_above, from_below, up[-1], down[-1]))
    up.append(around(u, 1))
    down.append(around(d, -1))
    far_up, far_down = around(u[:32], 2), around(d[32:], -2)
    attended2 = call(edge_attention_kernel, shape((BAND, WIDTH)), [VMEM] * 10, [], "edge_attention")(
        top_rows[0], top_rows[1], bottom_rows[0], bottom_rows[1], from_above, from_below, ga, w_qkv, bias, w_out
    )
    joined = call(edge_mlp_kernel, shape((4, 4 * MERGE_PAD, WIDTH)), [VMEM] * 6, [], "edge_mlp")(
        attended2, block1, gm, w_up, w_down, norm_merge.reshape(4, 1, WIDTH)
    )
    joined, far_up, far_down, up[-1], down[-1] = barrier((joined, far_up, far_down, up[-1], down[-1]))
    neighbour = lax.ppermute(joined, "lon", [(i, i ^ 1) for i in range(lon_count)])
    w_cols = [w_own, w_pair] + up + down + [far_up, far_down]
    own = call(merge_own_kernel, shape((16, MERGE_PAD, 128), F32), [VMEM] * 11, [], "merge_own")(joined, *w_cols)
    messages = call(
        merge_kernel,
        shape((16, 72, 128)),
        [VMEM] * 12,
        [pltpu.VMEM((16, 80, 128), F32)],
        "merge",
    )(neighbour, own, *w_cols)
    cores = [[2 * i + c for i in range(chips)] for c in range(2)]
    received = lax.all_to_all(messages, "lon", 0, 0, tiled=True, axis_index_groups=cores)
    out = call(unpack_kernel, shape((6, 128, 192)), [VMEM], [pltpu.VMEM((1160, 128), F32)],  "unpack")(received)
    return out.reshape(6, 4, 32, 192).transpose(0, 3, 1, 2)


def solution(mesh):
    in_specs = (P("lat", "lon", None, None), P(), P(), P(), P(), P(), P(), P(), P(), P(None, "lon"))
    out_specs = P("lat", None, None, "lon")
    return jax.shard_map(on_device, mesh=mesh, in_specs=in_specs, out_specs=out_specs, check_vma=False)
```

```python
import jax
import jax.numpy as jnp
from jax import lax
from jax.experimental import pallas as pl
from jax.experimental.pallas import tpu as pltpu
from jax.sharding import PartitionSpec as P

HEADS = 16
HEAD_DIM = 32
WIDTH = 512
FFN = 2048
ROWS = 12
HALF = 6
WIN = 144
HALF_WIN = 72
BAND = 288
LOG2E = 1.4426950408889634
EPS = 1e-05
BIG = -1e30
BF = jnp.bfloat16
F32 = jnp.float32
LEVELS = ((1, 2), (3, 0))
MERGE_PAD = 40
Z_STEPS = (0, -1, -2, -3, 1, 2, 3, 4)


def dot(a, b, dims=((1,), (0,))):
    return lax.dot_general(a, b, (dims, ((), ())), preferred_element_type=F32)


NT = ((1,), (1,))


def count_steps(value, starts):
    return sum((value >= start).astype(jnp.int32) for start in starts)


def one_hot(column, width):
    lane = lax.broadcasted_iota(jnp.int32, (column.shape[0], width), 1)
    return jnp.where(lane == column, 1.0, 0.0).astype(BF)


def row_numbers(count):
    return lax.broadcasted_iota(jnp.int32, (count, 1), 0)


def split_window(n):
    ihalf = count_steps(n, (72,))
    k = count_steps(n - 72 * ihalf, (36,))
    rest = n - 72 * ihalf - 36 * k
    i3 = count_steps(rest, (12, 24))
    return ihalf, k, i3, rest - 12 * i3


def bias_permutation():
    ihalf, k, i3, j = split_window(row_numbers(WIN))
    return one_hot(2 * (36 * ihalf + 12 * i3 + j) + k, WIN)


def band_places():
    n = row_numbers(BAND)
    t = count_steps(n, (WIN,))
    ihalf, k, i3, j = split_window(n - WIN * t)
    half = count_steps(j, (6,))
    level = jnp.where(t == 0, 1 + k, 3 - 3 * k)
    return half, ihalf, 24 * i3 + 4 * (j - 6 * half) + level


def merge_places(dj, di):
    n = row_numbers(4 * MERGE_PAD)
    level = count_steps(n, (MERGE_PAD, 2 * MERGE_PAD, 3 * MERGE_PAD))
    q = n - MERGE_PAD * level
    b = count_steps(q, (6, 12, 18, 24, 30))
    r, j = 2 * (q - 6 * b) + di, 2 * b + dj
    t = jnp.where((level == 0) | (level == 3), 1, 0)
    k = jnp.where((level == 0) | (level == 2), 1, 0)
    place = 36 * k + j
    ihalf = count_steps(r, (6,))
    band = count_steps(r, (9,))
    middle = 144 * t + 72 * ihalf + 12 * (r - 3 - 3 * ihalf) + place
    edge = 72 * (2 * band + t) + 12 * (r - 9 * band) + place
    inside = (r >= 3) & (r < 9)
    real = q < 36
    return jnp.where(real & inside, middle, -1), jnp.where(real & ~inside, edge, -1)


def normalise(x, gain):
    mean = jnp.sum(x, axis=-1, keepdims=True) * (1.0 / WIDTH)
    centred = x - mean
    spread = jnp.sum(centred * centred, axis=-1, keepdims=True) * (1.0 / WIDTH)
    return centred * lax.rsqrt(spread + EPS) * gain


def split3(x):
    hi = x.astype(BF)
    rest = x - hi.astype(F32)
    mid = rest.astype(BF)
    return hi, mid, (rest - mid.astype(F32)).astype(BF)


def split_kernel(tokens_hbm, right_out, left_out, right_ref, left_ref, sems):
    parts = ((right_ref, 0, right_out), (left_ref, HALF, left_out))
    copies = []
    for n, (held, start, _) in enumerate(parts):
        copies.append(pltpu.make_async_copy(tokens_hbm.at[:, start : start + HALF], held, sems.at[n]))
        copies[-1].start()
    for copy, (held, _, out) in zip(copies, parts):
        copy.wait()
        out[...] = held[...].astype(F32).reshape(BAND, WIDTH).astype(BF)


def prepare_kernel(bias_ref, bias_out, middle_out, edges_out, patches_out):
    perm = bias_permutation()
    for h in range(HEADS):
        parts = split3(bias_ref[h] * LOG2E)
        bias_out[h] = sum(dot(dot(perm, part).astype(BF), perm, NT) for part in parts)
    half, ihalf, place = band_places()
    for n in range(2):
        middle_out[n] = one_hot(jnp.where(half == n, 72 + 72 * ihalf + place, -1), BAND)
    for n in range(4):
        edges_out[n] = one_hot(jnp.where(2 * half + ihalf == n, place, -1), HALF_WIN)
    for p in range(4):
        middle, edge = merge_places(p // 2, p % 2)
        patches_out[p] = one_hot(jnp.where(middle >= 0, middle, jnp.where(edge >= 0, BAND + edge, -1)), 2 * BAND)


def attend_window(q, k, v, bias, kaug, qaug):
    count = q.shape[0]
    k, v = k.astype(BF), v.astype(BF)
    lane_head = lax.broadcasted_iota(jnp.int32, (count, 128), 1) // HEAD_DIM
    ones = jnp.ones((WIN, 128), BF)
    mixed = []
    for tile in range(4):
        lanes = slice(tile * 128, tile * 128 + 128)
        part = q[:, lanes]
        qm = jnp.concatenate([jnp.where(lane_head == n, part, 0.0) for n in range(4)], axis=0).astype(BF)
        s = dot(jnp.concatenate([qm, qaug], axis=1), jnp.concatenate([k[:, lanes], kaug], axis=1), NT) + bias(tile)
        p = jnp.exp2(s - jnp.max(s, axis=1, keepdims=True)).astype(BF)
        o = dot(p, jnp.concatenate([v[:, lanes], ones], axis=1))
        o = o[:, :128] * (1.0 / o[:, 128:])
        mixed.append(sum(jnp.where(lane_head == n, o[n * count : (n + 1) * count], 0.0) for n in range(4)))
    return jnp.concatenate(mixed, axis=1).astype(BF)


def feed_forward(attended, norm_mlp, up_ref, down_ref):
    normed = normalise(attended, norm_mlp).astype(BF)
    acc = attended
    step = 512
    for c in range(0, FFN, step):
        h = dot(normed, up_ref[:, c : c + step])
        h = 0.5 * h * (1.0 + lax.erf(h * 0.7071067811865476))
        acc = acc + dot(h.astype(BF), down_ref[c : c + step, :])
    return acc


def group_lanes(count):
    row = lax.broadcasted_iota(jnp.int32, (count, 128), 0)
    lane = lax.broadcasted_iota(jnp.int32, (count, 128), 1)
    return (row % HALF_WIN) // 36, row // HALF_WIN, lane


def middle_attention_kernel(left_ref, right_ref, perm_ref, ga_ref, wqkv_ref, bias_ref, wout_ref, out_ref):
    x = dot(perm_ref[0], left_ref[...]) + dot(perm_ref[1], right_ref[...])
    qkv = dot(normalise(x, ga_ref[...]).astype(BF), wqkv_ref[...])
    q = qkv[:, :WIDTH] * (LOG2E * HEAD_DIM**-0.5)
    group, _, lane = group_lanes(WIN)
    qgroup, _, qlane = group_lanes(4 * WIN)
    qaug = jnp.where(qlane == qgroup, 1.0, 0.0).astype(BF)

    def bias(tile):
        return jnp.concatenate([bias_ref[4 * tile + n] for n in range(4)], axis=0)

    pieces = []
    for t in range(2):
        rows = slice(t * WIN, (t + 1) * WIN)
        kaug = jnp.where((lane < 2) & (lane != group), BIG if t else 0.0, 0.0).astype(BF)
        pieces.append(attend_window(q[rows], qkv[rows, WIDTH : 2 * WIDTH], qkv[rows, 2 * WIDTH :], bias, kaug, qaug))
    update = dot(jnp.concatenate(pieces, axis=0), wout_ref[...])
    out_ref[...] = (x + update).astype(BF)


def middle_mlp_kernel(x_ref, gm_ref, up_ref, down_ref, out_ref):
    out_ref[...] = feed_forward(x_ref[...].astype(F32), gm_ref[...], up_ref, down_ref).astype(BF)


def edge_attention_kernel(
    lt_ref, rt_ref, lb_ref, rb_ref, top_ref, bottom_ref, perm_ref, ga_ref, wqkv_ref, bias_ref, wout_ref, out_ref
):
    bands = (
        (top_ref[0], lt_ref[...], top_ref[1], rt_ref[...]),
        (lb_ref[...], bottom_ref[0], rb_ref[...], bottom_ref[1]),
    )
    x = jnp.concatenate([sum(dot(perm_ref[n], piece) for n, piece in enumerate(band)) for band in bands], axis=0)
    normed = normalise(x, ga_ref[...])
    kv = dot(normed.astype(BF), wqkv_ref[:, WIDTH:])
    group, half, lane = group_lanes(WIN)
    qgroup, _, qlane = group_lanes(4 * HALF_WIN)
    qaug = jnp.where(qlane == qgroup, 1.0, 0.0).astype(BF)
    lat = lax.axis_index("lat")
    starts = [(n * 2 + t) * WIN + (1 - n) * HALF_WIN for n in range(2) for t in range(2)]
    asked = jnp.concatenate([normed[start : start + HALF_WIN] for start in starts], axis=0).astype(BF)
    q = dot(asked, wqkv_ref[:, :WIDTH]) * (LOG2E * HEAD_DIM**-0.5)
    pieces = []
    for w, start in enumerate(starts):
        n, t = w // 2, w % 2
        off = jnp.where(lat == (lax.axis_size("lat") - 1 if n else 0), BIG, 0.0)
        other = jnp.where(lane != group, BIG if t else 0.0, 0.0)
        kaug = jnp.where(lane < 2, jnp.where(half == n, jnp.minimum(off, other), other), 0.0).astype(BF)
        rows = slice(w * WIN, (w + 1) * WIN)

        def bias(tile):
            asked_rows = slice((1 - n) * HALF_WIN, (2 - n) * HALF_WIN)
            return jnp.concatenate([bias_ref[4 * tile + m, asked_rows, :] for m in range(4)], axis=0)

        mixed = attend_window(q[w * HALF_WIN : (w + 1) * HALF_WIN], kv[rows, :WIDTH], kv[rows, WIDTH:], bias, kaug, qaug)
        pieces.append(mixed.astype(F32))
    update = dot(jnp.concatenate(pieces, axis=0).astype(BF), wout_ref[...])
    kept = jnp.concatenate([x[start : start + HALF_WIN] for start in starts], axis=0)
    out_ref[...] = (kept + update).astype(BF)


def edge_mlp_kernel(x_ref, blk1_ref, gm_ref, up_ref, down_ref, gg_ref, patches_ref, out_ref):
    block = feed_forward(x_ref[...].astype(F32), gm_ref[...], up_ref, down_ref).astype(BF)
    blocks = jnp.concatenate([blk1_ref[...], block], axis=0)
    patches = [dot(patches_ref[p], blocks) for p in range(4)]
    mean = sum(jnp.sum(v, axis=-1, keepdims=True) for v in patches) * (1.0 / (4 * WIDTH))
    centred = [v - mean for v in patches]
    spread = sum(jnp.sum(v * v, axis=-1, keepdims=True) for v in centred) * (1.0 / (4 * WIDTH))
    scale = lax.rsqrt(spread + EPS)
    for p in range(4):
        out_ref[p] = (centred[p] * scale * gg_ref[p]).astype(BF)


def merge_columns(joined_ref, w_refs):
    chunk = lax.broadcasted_iota(jnp.int32, (MERGE_PAD, 128), 1) // 32
    messages = []
    for part in (w_refs[:5], w_refs[5:]):
        total = 0.0
        for p in range(4):
            lanes = slice(p * WIDTH, (p + 1) * WIDTH)
            total = total + dot(joined_ref[p], jnp.concatenate([r[:, lanes] for r in part], axis=0), NT)
        for tile in range(2):
            levels = [
                total[lev * MERGE_PAD : (lev + 1) * MERGE_PAD, tile * 128 : (tile + 1) * 128] for lev in range(4)
            ]
            for d in range(4):
                value = jnp.zeros((MERGE_PAD, 128), F32)
                for lev in range(4):
                    shift = (lev - d) % 4 * 32
                    moved = pltpu.roll(levels[lev], shift, 1) if shift else levels[lev]
                    value = jnp.where(chunk == lev, moved, value)
                messages.append(value)
    return messages


def merge_own_kernel(joined_ref, *refs):
    for block, value in enumerate(merge_columns(joined_ref, refs[:-1])):
        refs[-1][block] = value


def merge_kernel(joined_ref, own_ref, *refs):
    w_refs, (out_ref, message_ref) = refs[:-2], refs[-2:]
    lon = lax.axis_index("lon")
    chips = lax.axis_size("lon") // 2
    first = lax.rem(lon, 2) == 0
    z = lax.rem(lon // 2, 8)
    y = lon // chips
    for block, other in enumerate(merge_columns(joined_ref, w_refs)):
        own = own_ref[block]
        message_ref[block, :MERGE_PAD] = jnp.where(first, own, other)
        message_ref[block, 36 : 36 + MERGE_PAD] = jnp.where(first, other, own)
        zd = lax.rem(z + Z_STEPS[block // 2] + 8, 8)
        yd = 1 - y if block % 2 else y
        out_ref[yd * 8 + zd] = message_ref[block, :72].astype(BF)


def unpack_kernel(in_ref, out_ref, rows_ref):
    for n in range(16):
        rows_ref[n * 72 : (n + 1) * 72, :] = in_ref[n].astype(F32)
    for a in range(6):
        piece = rows_ref[pl.ds(a, 192, stride=6), :]
        out_ref[a] = pltpu.roll(piece, 3, 0).T.astype(BF)


VMEM = pl.BlockSpec(memory_space=pltpu.VMEM)
ANY = pl.BlockSpec(memory_space=pl.ANY)


def call(kernel, out_shape, in_specs, scratch, name, limit=28):
    out_specs = jax.tree.map(lambda _: VMEM, out_shape)
    return pl.pallas_call(
        kernel,
        out_shape=out_shape,
        in_specs=in_specs,
        out_specs=out_specs,
        scratch_shapes=scratch,
        compiler_params=pltpu.CompilerParams(vmem_limit_bytes=limit << 20),
        cost_estimate=pl.CostEstimate(flops=1 << 20, bytes_accessed=1 << 16, transcendentals=0),
        name=name,
    )


def on_device(tokens, norm_attn, w_qkv, pos_bias, w_out, norm_mlp, w_up, w_down, norm_merge, w_merge):
    shape = lambda s, d=BF: jax.ShapeDtypeStruct(s, d)
    barrier = lax.optimization_barrier
    lat_count = lax.axis_size("lat")
    lon_count = lax.axis_size("lon")
    chips = lon_count // 2
    held = pltpu.VMEM((ROWS, HALF, 4, WIDTH), BF)

    def around(block, step):
        route = []
        for i in range(lon_count):
            y, z, c = i // chips, i // 2 % 8, i % 2
            route.append((i, y * chips + (z + step) % 8 * 2 + c))
        return lax.ppermute(block, "lon", route)

    w_own = w_merge.T
    w_pair = lax.ppermute(w_own, "lon", [(i, (i + chips) % lon_count) for i in range(lon_count)])
    right_own, left = call(
        split_kernel, (shape((BAND, WIDTH)),) * 2, [ANY], [held, held, pltpu.SemaphoreType.DMA((2,))], "split", 28
    )(tokens)
    right = lax.ppermute(right_own, "lon", [((i + 1) % lon_count, i) for i in range(lon_count)])
    own_up, own_down = around(w_own, 1), around(w_own, -1)
    w_pair, pos_bias = barrier((w_pair, pos_bias))
    pair_up, pair_down = around(w_pair, 1), around(w_pair, -1)
    made = (
        shape((HEADS, WIN, WIN), F32),
        shape((2, BAND, BAND)),
        shape((4, BAND, HALF_WIN)),
        shape((4, 4 * MERGE_PAD, 2 * BAND)),
    )
    bias, middle_perm, edge_perm, patch_perm = call(prepare_kernel, made, [VMEM], [], "prepare")(pos_bias)

    bias, right, own_up, own_down, pair_up, pair_down = barrier((bias, right, own_up, own_down, pair_up, pair_down))
    up, down = [jnp.concatenate([own_up, pair_up], axis=0)], [jnp.concatenate([own_down, pair_down], axis=0)]
    up.append(around(up[-1], 1))
    down.append(around(down[-1], -1))
    top_rows = jnp.stack([left[:HALF_WIN], right[:HALF_WIN]])
    bottom_rows = jnp.stack([left[-HALF_WIN:], right[-HALF_WIN:]])
    from_above = lax.ppermute(bottom_rows, "lat", [(i, i + 1) for i in range(lat_count - 1)])
    from_below = lax.ppermute(top_rows, "lat", [(i + 1, i) for i in range(lat_count - 1)])
    ga, gm = norm_attn.reshape(1, WIDTH), norm_mlp.reshape(1, WIDTH)
    attended1 = call(middle_attention_kernel, shape((BAND, WIDTH)), [VMEM] * 7, [], "middle_attention")(
        left, right, middle_perm, ga, w_qkv, bias, w_out
    )
    block1 = call(middle_mlp_kernel, shape((BAND, WIDTH)), [VMEM] * 4, [], "middle_mlp")(attended1, gm, w_up, w_down)

    block1, from_above, from_below, u, d = barrier((block1, from_above, from_below, up[-1], down[-1]))
    up.append(around(u, 1))
    down.append(around(d, -1))
    far_up, far_down = around(u[:32], 2), around(d[32:], -2)
    attended2 = call(edge_attention_kernel, shape((BAND, WIDTH)), [VMEM] * 11, [], "edge_attention")(
        top_rows[0], top_rows[1], bottom_rows[0], bottom_rows[1], from_above, from_below, edge_perm, ga, w_qkv, bias, w_out
    )
    joined = call(edge_mlp_kernel, shape((4, 4 * MERGE_PAD, WIDTH)), [VMEM] * 7, [], "edge_mlp")(
        attended2, block1, gm, w_up, w_down, norm_merge.reshape(4, 1, WIDTH), patch_perm
    )
    joined, far_up, far_down, up[-1], down[-1] = barrier((joined, far_up, far_down, up[-1], down[-1]))
    neighbour = lax.ppermute(joined, "lon", [(i, i ^ 1) for i in range(lon_count)])
    w_cols = [w_own, w_pair] + up + down + [far_up, far_down]
    own = call(merge_own_kernel, shape((16, MERGE_PAD, 128), F32), [VMEM] * 11, [], "merge_own")(joined, *w_cols)
    messages = call(
        merge_kernel,
        shape((16, 72, 128)),
        [VMEM] * 12,
        [pltpu.VMEM((16, 80, 128), F32)],
        "merge",
    )(neighbour, own, *w_cols)
    cores = [[2 * i + c for i in range(chips)] for c in range(2)]
    received = lax.all_to_all(messages, "lon", 0, 0, tiled=True, axis_index_groups=cores)
    out = call(unpack_kernel, shape((6, 128, 192)), [VMEM], [pltpu.VMEM((1160, 128), F32)],  "unpack")(received)
    return out.reshape(6, 4, 32, 192).transpose(0, 3, 1, 2)


def solution(mesh):
    in_specs = (P("lat", "lon", None, None), P(), P(), P(), P(), P(), P(), P(), P(), P(None, "lon"))
    out_specs = P("lat", None, None, "lon")
    return jax.shard_map(on_device, mesh=mesh, in_specs=in_specs, out_specs=out_specs, check_vma=False)
```

```python
import jax
import jax.numpy as jnp
from jax import lax
from jax.experimental import pallas as pl
from jax.experimental.pallas import tpu as pltpu
from jax.sharding import PartitionSpec as P

HEADS = 16
HEAD_DIM = 32
WIDTH = 512
FFN = 2048
ROWS = 12
HALF = 6
WIN = 144
HALF_WIN = 72
BAND = 288
LOG2E = 1.4426950408889634
EPS = 1e-05
BIG = -1e30
BF = jnp.bfloat16
F32 = jnp.float32
LEVELS = ((1, 2), (3, 0))
MERGE_PAD = 40
Z_STEPS = (0, -1, -2, -3, 1, 2, 3, 4)


def dot(a, b, dims=((1,), (0,))):
    return lax.dot_general(a, b, (dims, ((), ())), preferred_element_type=F32)


NT = ((1,), (1,))


def count_steps(value, starts):
    return sum((value >= start).astype(jnp.int32) for start in starts)


def one_hot(column, width):
    lane = lax.broadcasted_iota(jnp.int32, (column.shape[0], width), 1)
    return jnp.where(lane == column, 1.0, 0.0).astype(BF)


def row_numbers(count):
    return lax.broadcasted_iota(jnp.int32, (count, 1), 0)


def split_window(n):
    ihalf = count_steps(n, (72,))
    k = count_steps(n - 72 * ihalf, (36,))
    rest = n - 72 * ihalf - 36 * k
    i3 = count_steps(rest, (12, 24))
    return ihalf, k, i3, rest - 12 * i3


def bias_permutation():
    ihalf, k, i3, j = split_window(row_numbers(WIN))
    return one_hot(2 * (36 * ihalf + 12 * i3 + j) + k, WIN)


def band_places():
    n = row_numbers(BAND)
    t = count_steps(n, (WIN,))
    ihalf, k, i3, j = split_window(n - WIN * t)
    half = count_steps(j, (6,))
    level = jnp.where(t == 0, 1 + k, 3 - 3 * k)
    return half, ihalf, 24 * i3 + 4 * (j - 6 * half) + level


def merge_places(dj, di):
    n = row_numbers(4 * MERGE_PAD)
    level = count_steps(n, (MERGE_PAD, 2 * MERGE_PAD, 3 * MERGE_PAD))
    q = n - MERGE_PAD * level
    b = count_steps(q, (6, 12, 18, 24, 30))
    r, j = 2 * (q - 6 * b) + di, 2 * b + dj
    t = jnp.where((level == 0) | (level == 3), 1, 0)
    k = jnp.where((level == 0) | (level == 2), 1, 0)
    place = 36 * k + j
    ihalf = count_steps(r, (6,))
    band = count_steps(r, (9,))
    middle = 144 * t + 72 * ihalf + 12 * (r - 3 - 3 * ihalf) + place
    edge = 72 * (2 * band + t) + 12 * (r - 9 * band) + place
    inside = (r >= 3) & (r < 9)
    real = q < 36
    return jnp.where(real & inside, middle, -1), jnp.where(real & ~inside, edge, -1)


def normalise(x, gain):
    mean = jnp.sum(x, axis=-1, keepdims=True) * (1.0 / WIDTH)
    centred = x - mean
    spread = jnp.sum(centred * centred, axis=-1, keepdims=True) * (1.0 / WIDTH)
    return centred * lax.rsqrt(spread + EPS) * gain


def split3(x):
    hi = x.astype(BF)
    rest = x - hi.astype(F32)
    mid = rest.astype(BF)
    return hi, mid, (rest - mid.astype(F32)).astype(BF)


def split_kernel(tokens_hbm, right_out, left_out, right_ref, left_ref, sems):
    parts = ((right_ref, 0, right_out), (left_ref, HALF, left_out))
    copies = []
    for n, (held, start, _) in enumerate(parts):
        copies.append(pltpu.make_async_copy(tokens_hbm.at[:, start : start + HALF], held, sems.at[n]))
        copies[-1].start()
    for copy, (held, _, out) in zip(copies, parts):
        copy.wait()
        out[...] = held[...].astype(F32).reshape(BAND, WIDTH).astype(BF)


def prepare_kernel(bias_ref, bias_out, middle_out, edges_out, patches_out):
    perm = bias_permutation()
    for h in range(HEADS):
        parts = split3(bias_ref[h] * LOG2E)
        bias_out[h] = sum(dot(dot(perm, part).astype(BF), perm, NT) for part in parts)
    half, ihalf, place = band_places()
    for n in range(2):
        middle_out[n] = one_hot(jnp.where(half == n, 72 + 72 * ihalf + place, -1), BAND)
    for n in range(4):
        edges_out[n] = one_hot(jnp.where(2 * half + ihalf == n, place, -1), HALF_WIN)
    for p in range(4):
        middle, edge = merge_places(p // 2, p % 2)
        patches_out[p] = one_hot(jnp.where(middle >= 0, middle, jnp.where(edge >= 0, BAND + edge, -1)), 2 * BAND)


def attend_window(q, k, v, bias, kaug, qaug):
    count = q.shape[0]
    k, v = k.astype(BF), v.astype(BF)
    lane_head = lax.broadcasted_iota(jnp.int32, (count, 128), 1) // HEAD_DIM
    ones = jnp.ones((WIN, 128), BF)
    mixed = []
    for tile in range(4):
        lanes = slice(tile * 128, tile * 128 + 128)
        part = q[:, lanes]
        qm = jnp.concatenate([jnp.where(lane_head == n, part, 0.0) for n in range(4)], axis=0).astype(BF)
        s = dot(jnp.concatenate([qm, qaug], axis=1), jnp.concatenate([k[:, lanes], kaug], axis=1), NT) + bias(tile)
        p = jnp.exp2(s - jnp.max(s, axis=1, keepdims=True)).astype(BF)
        o = dot(p, jnp.concatenate([v[:, lanes], ones], axis=1))
        o = o[:, :128] * (1.0 / o[:, 128:])
        mixed.append(sum(jnp.where(lane_head == n, o[n * count : (n + 1) * count], 0.0) for n in range(4)))
    return jnp.concatenate(mixed, axis=1).astype(BF)


def feed_forward(attended, norm_mlp, up_ref, down_ref):
    normed = normalise(attended, norm_mlp).astype(BF)
    acc = attended
    step = 1024
    for c in range(0, FFN, step):
        h = dot(normed, up_ref[:, c : c + step])
        h = 0.5 * h * (1.0 + lax.erf(h * 0.7071067811865476))
        acc = acc + dot(h.astype(BF), down_ref[c : c + step, :])
    return acc


def group_lanes(count):
    row = lax.broadcasted_iota(jnp.int32, (count, 128), 0)
    lane = lax.broadcasted_iota(jnp.int32, (count, 128), 1)
    return (row % HALF_WIN) // 36, row // HALF_WIN, lane


def middle_attention_kernel(left_ref, right_ref, perm_ref, ga_ref, wqkv_ref, bias_ref, wout_ref, out_ref):
    x = dot(perm_ref[0], left_ref[...]) + dot(perm_ref[1], right_ref[...])
    qkv = dot(normalise(x, ga_ref[...]).astype(BF), wqkv_ref[...])
    q = qkv[:, :WIDTH] * (LOG2E * HEAD_DIM**-0.5)
    group, _, lane = group_lanes(WIN)
    qgroup, _, qlane = group_lanes(4 * WIN)
    qaug = jnp.where(qlane == qgroup, 1.0, 0.0).astype(BF)

    def bias(tile):
        return jnp.concatenate([bias_ref[4 * tile + n] for n in range(4)], axis=0)

    pieces = []
    for t in range(2):
        rows = slice(t * WIN, (t + 1) * WIN)
        kaug = jnp.where((lane < 2) & (lane != group), BIG if t else 0.0, 0.0).astype(BF)
        pieces.append(attend_window(q[rows], qkv[rows, WIDTH : 2 * WIDTH], qkv[rows, 2 * WIDTH :], bias, kaug, qaug))
    update = dot(jnp.concatenate(pieces, axis=0), wout_ref[...])
    out_ref[...] = (x + update).astype(BF)


def middle_mlp_kernel(x_ref, gm_ref, up_ref, down_ref, out_ref):
    out_ref[...] = feed_forward(x_ref[...].astype(F32), gm_ref[...], up_ref, down_ref).astype(BF)


def edge_attention_kernel(
    lt_ref, rt_ref, lb_ref, rb_ref, top_ref, bottom_ref, perm_ref, ga_ref, wqkv_ref, bias_ref, wout_ref, out_ref
):
    bands = (
        (top_ref[0], lt_ref[...], top_ref[1], rt_ref[...]),
        (lb_ref[...], bottom_ref[0], rb_ref[...], bottom_ref[1]),
    )
    x = jnp.concatenate([sum(dot(perm_ref[n], piece) for n, piece in enumerate(band)) for band in bands], axis=0)
    normed = normalise(x, ga_ref[...])
    kv = dot(normed.astype(BF), wqkv_ref[:, WIDTH:])
    group, half, lane = group_lanes(WIN)
    qgroup, _, qlane = group_lanes(4 * HALF_WIN)
    qaug = jnp.where(qlane == qgroup, 1.0, 0.0).astype(BF)
    lat = lax.axis_index("lat")
    starts = [(n * 2 + t) * WIN + (1 - n) * HALF_WIN for n in range(2) for t in range(2)]
    asked = jnp.concatenate([normed[start : start + HALF_WIN] for start in starts], axis=0).astype(BF)
    q = dot(asked, wqkv_ref[:, :WIDTH]) * (LOG2E * HEAD_DIM**-0.5)
    pieces = []
    for w, start in enumerate(starts):
        n, t = w // 2, w % 2
        off = jnp.where(lat == (lax.axis_size("lat") - 1 if n else 0), BIG, 0.0)
        other = jnp.where(lane != group, BIG if t else 0.0, 0.0)
        kaug = jnp.where(lane < 2, jnp.where(half == n, jnp.minimum(off, other), other), 0.0).astype(BF)
        rows = slice(w * WIN, (w + 1) * WIN)

        def bias(tile):
            asked_rows = slice((1 - n) * HALF_WIN, (2 - n) * HALF_WIN)
            return jnp.concatenate([bias_ref[4 * tile + m, asked_rows, :] for m in range(4)], axis=0)

        mixed = attend_window(q[w * HALF_WIN : (w + 1) * HALF_WIN], kv[rows, :WIDTH], kv[rows, WIDTH:], bias, kaug, qaug)
        pieces.append(mixed.astype(F32))
    update = dot(jnp.concatenate(pieces, axis=0).astype(BF), wout_ref[...])
    kept = jnp.concatenate([x[start : start + HALF_WIN] for start in starts], axis=0)
    out_ref[...] = (kept + update).astype(BF)


def edge_mlp_kernel(x_ref, blk1_ref, gm_ref, up_ref, down_ref, gg_ref, patches_ref, out_ref):
    block = feed_forward(x_ref[...].astype(F32), gm_ref[...], up_ref, down_ref).astype(BF)
    blocks = jnp.concatenate([blk1_ref[...], block], axis=0)
    patches = [dot(patches_ref[p], blocks) for p in range(4)]
    mean = sum(jnp.sum(v, axis=-1, keepdims=True) for v in patches) * (1.0 / (4 * WIDTH))
    centred = [v - mean for v in patches]
    spread = sum(jnp.sum(v * v, axis=-1, keepdims=True) for v in centred) * (1.0 / (4 * WIDTH))
    scale = lax.rsqrt(spread + EPS)
    for p in range(4):
        out_ref[p] = (centred[p] * scale * gg_ref[p]).astype(BF)


def merge_columns(joined_ref, w_refs):
    chunk = lax.broadcasted_iota(jnp.int32, (MERGE_PAD, 128), 1) // 32
    messages = []
    for part in (w_refs[:5], w_refs[5:]):
        total = 0.0
        for p in range(4):
            lanes = slice(p * WIDTH, (p + 1) * WIDTH)
            total = total + dot(joined_ref[p], jnp.concatenate([r[:, lanes] for r in part], axis=0), NT)
        for tile in range(2):
            levels = [
                total[lev * MERGE_PAD : (lev + 1) * MERGE_PAD, tile * 128 : (tile + 1) * 128] for lev in range(4)
            ]
            for d in range(4):
                value = jnp.zeros((MERGE_PAD, 128), F32)
                for lev in range(4):
                    shift = (lev - d) % 4 * 32
                    moved = pltpu.roll(levels[lev], shift, 1) if shift else levels[lev]
                    value = jnp.where(chunk == lev, moved, value)
                messages.append(value)
    return messages


def merge_own_kernel(joined_ref, *refs):
    for block, value in enumerate(merge_columns(joined_ref, refs[:-1])):
        refs[-1][block] = value


def merge_kernel(joined_ref, own_ref, *refs):
    w_refs, (out_ref, message_ref) = refs[:-2], refs[-2:]
    lon = lax.axis_index("lon")
    chips = lax.axis_size("lon") // 2
    first = lax.rem(lon, 2) == 0
    z = lax.rem(lon // 2, 8)
    y = lon // chips
    for block, other in enumerate(merge_columns(joined_ref, w_refs)):
        own = own_ref[block]
        message_ref[block, :MERGE_PAD] = jnp.where(first, own, other)
        message_ref[block, 36 : 36 + MERGE_PAD] = jnp.where(first, other, own)
        zd = lax.rem(z + Z_STEPS[block // 2] + 8, 8)
        yd = 1 - y if block % 2 else y
        out_ref[yd * 8 + zd] = message_ref[block, :72].astype(BF)


def unpack_kernel(in_ref, out_ref, rows_ref):
    for n in range(16):
        rows_ref[n * 72 : (n + 1) * 72, :] = in_ref[n].astype(F32)
    for a in range(6):
        piece = rows_ref[pl.ds(a, 192, stride=6), :]
        out_ref[a] = pltpu.roll(piece, 3, 0).T.astype(BF)


VMEM = pl.BlockSpec(memory_space=pltpu.VMEM)
ANY = pl.BlockSpec(memory_space=pl.ANY)


def call(kernel, out_shape, in_specs, scratch, name, limit=28):
    out_specs = jax.tree.map(lambda _: VMEM, out_shape)
    return pl.pallas_call(
        kernel,
        out_shape=out_shape,
        in_specs=in_specs,
        out_specs=out_specs,
        scratch_shapes=scratch,
        compiler_params=pltpu.CompilerParams(vmem_limit_bytes=limit << 20),
        cost_estimate=pl.CostEstimate(flops=1 << 20, bytes_accessed=1 << 16, transcendentals=0),
        name=name,
    )


def on_device(tokens, norm_attn, w_qkv, pos_bias, w_out, norm_mlp, w_up, w_down, norm_merge, w_merge):
    shape = lambda s, d=BF: jax.ShapeDtypeStruct(s, d)
    barrier = lax.optimization_barrier
    lat_count = lax.axis_size("lat")
    lon_count = lax.axis_size("lon")
    chips = lon_count // 2
    held = pltpu.VMEM((ROWS, HALF, 4, WIDTH), BF)

    def around(block, step):
        route = []
        for i in range(lon_count):
            y, z, c = i // chips, i // 2 % 8, i % 2
            route.append((i, y * chips + (z + step) % 8 * 2 + c))
        return lax.ppermute(block, "lon", route)

    w_own = w_merge.T
    w_pair = lax.ppermute(w_own, "lon", [(i, (i + chips) % lon_count) for i in range(lon_count)])
    right_own, left = call(
        split_kernel, (shape((BAND, WIDTH)),) * 2, [ANY], [held, held, pltpu.SemaphoreType.DMA((2,))], "split", 28
    )(tokens)
    right = lax.ppermute(right_own, "lon", [((i + 1) % lon_count, i) for i in range(lon_count)])
    own_up, own_down = around(w_own, 1), around(w_own, -1)
    w_pair, pos_bias = barrier((w_pair, pos_bias))
    pair_up, pair_down = around(w_pair, 1), around(w_pair, -1)
    made = (
        shape((HEADS, WIN, WIN), F32),
        shape((2, BAND, BAND)),
        shape((4, BAND, HALF_WIN)),
        shape((4, 4 * MERGE_PAD, 2 * BAND)),
    )
    bias, middle_perm, edge_perm, patch_perm = call(prepare_kernel, made, [VMEM], [], "prepare")(pos_bias)

    bias, right, own_up, own_down, pair_up, pair_down = barrier((bias, right, own_up, own_down, pair_up, pair_down))
    up, down = [jnp.concatenate([own_up, pair_up], axis=0)], [jnp.concatenate([own_down, pair_down], axis=0)]
    up.append(around(up[-1], 1))
    down.append(around(down[-1], -1))
    top_rows = jnp.stack([left[:HALF_WIN], right[:HALF_WIN]])
    bottom_rows = jnp.stack([left[-HALF_WIN:], right[-HALF_WIN:]])
    from_above = lax.ppermute(bottom_rows, "lat", [(i, i + 1) for i in range(lat_count - 1)])
    from_below = lax.ppermute(top_rows, "lat", [(i + 1, i) for i in range(lat_count - 1)])
    ga, gm = norm_attn.reshape(1, WIDTH), norm_mlp.reshape(1, WIDTH)
    attended1 = call(middle_attention_kernel, shape((BAND, WIDTH)), [VMEM] * 7, [], "middle_attention")(
        left, right, middle_perm, ga, w_qkv, bias, w_out
    )
    block1 = call(middle_mlp_kernel, shape((BAND, WIDTH)), [VMEM] * 4, [], "middle_mlp")(attended1, gm, w_up, w_down)

    block1, from_above, from_below, u, d = barrier((block1, from_above, from_below, up[-1], down[-1]))
    up.append(around(u, 1))
    down.append(around(d, -1))
    far_up, far_down = around(u[:32], 2), around(d[32:], -2)
    attended2 = call(edge_attention_kernel, shape((BAND, WIDTH)), [VMEM] * 11, [], "edge_attention")(
        top_rows[0], top_rows[1], bottom_rows[0], bottom_rows[1], from_above, from_below, edge_perm, ga, w_qkv, bias, w_out
    )
    joined = call(edge_mlp_kernel, shape((4, 4 * MERGE_PAD, WIDTH)), [VMEM] * 7, [], "edge_mlp")(
        attended2, block1, gm, w_up, w_down, norm_merge.reshape(4, 1, WIDTH), patch_perm
    )
    joined, far_up, far_down, up[-1], down[-1] = barrier((joined, far_up, far_down, up[-1], down[-1]))
    neighbour = lax.ppermute(joined, "lon", [(i, i ^ 1) for i in range(lon_count)])
    w_cols = [w_own, w_pair] + up + down + [far_up, far_down]
    own = call(merge_own_kernel, shape((16, MERGE_PAD, 128), F32), [VMEM] * 11, [], "merge_own")(joined, *w_cols)
    messages = call(
        merge_kernel,
        shape((16, 72, 128)),
        [VMEM] * 12,
        [pltpu.VMEM((16, 80, 128), F32)],
        "merge",
    )(neighbour, own, *w_cols)
    cores = [[2 * i + c for i in range(chips)] for c in range(2)]
    received = lax.all_to_all(messages, "lon", 0, 0, tiled=True, axis_index_groups=cores)
    out = call(unpack_kernel, shape((6, 128, 192)), [VMEM], [pltpu.VMEM((1160, 128), F32)],  "unpack")(received)
    return out.reshape(6, 4, 32, 192).transpose(0, 3, 1, 2)


def solution(mesh):
    in_specs = (P("lat", "lon", None, None), P(), P(), P(), P(), P(), P(), P(), P(), P(None, "lon"))
    out_specs = P("lat", None, None, "lon")
    return jax.shard_map(on_device, mesh=mesh, in_specs=in_specs, out_specs=out_specs, check_vma=False)
```
